256 devices in a mesh: group: 2 (over core), ctx: 8 (over z), tp: 16 (over y, x).
Axes of the slice: x: 4, y: 4, z: 8, core: 2. Of those that a mesh axis runs over, the one named last changes fastest.
Arguments:
- hidden: bfloat16 [2, 1024, 8192], P('group', 'ctx', 'tp'), may hold values from -6 to 6
- queries: bfloat16 [2, 1024, 4096], P('group', 'ctx', 'tp'), may hold values from -400 to 400
- kv_weight: bfloat16 [8192, 2048], P(None, 'tp'), may hold values from -0.0625 to 0.0625
- out_weight: bfloat16 [4096, 8192], P('tp'), may hold values from -0.375 to 0.375
- cache: bfloat16 [1024, 128, 4096], P('ctx', None, 'tp'), may hold values from -6 to 6
- page_owner: int32 [128], replicated, may hold values from 0 to 7, as said below
- page_slot: int32 [128], replicated, may hold values from 0 to 1023, as said below
- cached_len: int32 [1024], P('ctx'), may hold values from 64 to 128
Outputs:
- layer_out: bfloat16 [2, 1024, 8192], P('group', 'ctx')
The draws below stay inside these ranges and needn't reach their ends.
Inputs may be any that keep to these rules, and one draw needn't show every extreme that they name: `page_owner`: each aligned block of 16 entries belongs to one prefill context shard; within a block no owner appears more than 2 times, and some owner appears exactly 2 times in every block; in the last block that owner is 0. `page_slot`: all slots differ; slot s is page s % 8 of request s // 8 among the owner's 128 requests.
All inputs are finite; a program needn't handle non-finite values.
Results may differ from the reference program's by a relative error of at most 0.012.
The reference program's roundings to bfloat16 on the way count: a program that leaves them out, or rounds other values in their place, can miss the bound.
Values may be sent and summed in bfloat16 or wider, within the bound.
No kernel may reach another device: no remote copies, remote signals or barrier semaphores. Data moves between devices by JAX's collectives and lax.ppermute only.
A program may use at most 128 MiB of HBM per device.

```python
import math
import jax
import jax.numpy as jnp
from jax import lax

D = 8192
KVH = 8
HD = 128
HQ = 32
ROWS_DEV = 128
CL = 128
PAGE = 8
ROWS = 1024
NPAGE = 128
DEV_PAGES = 16
COPIES = 16
REQ_PAGES = 16
HALF_PAGES = 8
N_CTX = 8


def draw_queries(key, part):
    key = jax.random.fold_in(key, 11)
    base_key, spread_key = jax.random.split(key)
    base = jax.random.normal(base_key, (2, ROWS, HQ, HD), jnp.float32)
    spread = jnp.exp(jax.random.uniform(spread_key, (2, ROWS, HQ, 1), jnp.float32, math.log(0.5), math.log(2.0)))
    return jnp.clip(base * spread, -400.0, 400.0).reshape(2, ROWS, HQ * HD).astype(jnp.bfloat16)


def draw_page_owner(key, part):
    key = jax.random.fold_in(key, 23)

    def one_shard(shard_key, shard_index):
        order_key, mixing_key = jax.random.split(shard_key)
        order = jax.random.permutation(order_key, 2 * N_CTX)
        paired = jnp.where(shard_index == N_CTX - 1, 0, order[0] // 2)
        others = order[jnp.argsort((order // 2 == paired).astype(jnp.int32), stable=True)] // 2
        chosen = jnp.concatenate([jnp.stack([paired, paired]), others[:DEV_PAGES - 2]])
        return jax.random.permutation(mixing_key, chosen)
    shard_keys = jax.random.split(key, N_CTX)
    owners = jax.vmap(one_shard)(shard_keys, jnp.arange(N_CTX))
    return owners.reshape(NPAGE).astype(jnp.int32)


def draw_page_slot(key, part):
    key = jax.random.fold_in(key, 37)
    order_key, mixing_key = jax.random.split(key)
    slot_total = ROWS_DEV * HALF_PAGES
    order = jax.random.permutation(order_key, slot_total)
    upper = jnp.argmax(order == slot_total - 1)
    order = order.at[upper].set(order[0]).at[0].set(slot_total - 1)
    lower = jnp.argmax(order == 0)
    order = order.at[lower].set(order[1]).at[1].set(0)
    return jax.random.permutation(mixing_key, order[:NPAGE]).astype(jnp.int32)


def draw_cached_len(key, part):
    key = jax.random.fold_in(key, 41)
    length_key, pick_key = jax.random.split(key)
    lengths = jax.random.randint(length_key, (ROWS,), CL // 2, CL + 1)
    picks = jax.random.permutation(pick_key, ROWS)
    lengths = jnp.where(jnp.arange(ROWS) == picks[0], CL, lengths)
    lengths = jnp.where(jnp.arange(ROWS) == picks[1], CL // 2, lengths)
    return lengths.astype(jnp.int32)


def shard_levels(rng, dims, shards, smallest, top_value):
    gain, own = 1.0, jax.random.fold_in(rng, 6)
    for axis_at, blocks in shards:
        heights = jnp.exp(jax.random.uniform(jax.random.fold_in(own, axis_at), (blocks,), jnp.float32, smallest / len(shards), top_value / len(shards)))
        gain = gain * jnp.repeat(heights, dims[axis_at] // blocks).reshape([-1 if axis == axis_at else 1 for axis in range(len(dims))])
    return gain


def normal_values(own_key, dims, deviation, bound, cuts=(), kind=jnp.bfloat16):
    drawn = deviation * jax.random.normal(own_key, dims, jnp.float32)
    if cuts:
        drawn = drawn * shard_levels(own_key, dims, cuts, -0.22, 0.18)
    return jnp.clip(drawn, -bound, bound).astype(kind)


def setup_inputs(seed: int = 0) -> dict:
    splits = jax.random.split(jax.random.key(seed), 9)
    hidden = normal_values(splits[0], (2, ROWS, D), 1.0, 6.0, ((0, 2), (1, 8), (2, 16)))
    queries = draw_queries(jax.random.fold_in(splits[8], 71), 0)
    kv_weight = normal_values(splits[2], (D, KVH * 2 * HD), D ** -0.5, 0.0625, ((1, 16),))
    out_weight = normal_values(splits[3], (HQ * HD, D), (HQ * HD // 16) ** -0.5, 0.375, ((0, 16),))
    cache = normal_values(splits[4], (ROWS, CL, COPIES * 2 * HD), 1.0, 6.0, ((0, 8), (2, 16)))
    page_owner = draw_page_owner(jax.random.fold_in(splits[8], 71), 0)
    page_slot = draw_page_slot(jax.random.fold_in(splits[8], 71), 0)
    cached_len = draw_cached_len(jax.random.fold_in(splits[8], 71), 0)
    return {"hidden": hidden, "queries": queries, "kv_weight": kv_weight, "out_weight": out_weight, "cache": cache, "page_owner": page_owner, "page_slot": page_slot, "cached_len": cached_len}


def project_parts(hidden, kv_weight):
    prefill_kv = jnp.dot(hidden[0], kv_weight, preferred_element_type=jnp.float32).astype(jnp.bfloat16)
    decode_kv = jnp.dot(hidden[1], kv_weight, preferred_element_type=jnp.float32).astype(jnp.bfloat16)
    return prefill_kv, decode_kv


def span_attention(span_queries, prefill_kv):
    groups = HQ // COPIES
    copy_head = (jnp.arange(COPIES) * KVH) // COPIES
    query_rows = span_queries.reshape(ROWS, COPIES, groups, HD).astype(jnp.float32)
    keyed = prefill_kv.reshape(ROWS, KVH, 2, HD)[:, copy_head].astype(jnp.float32)
    scores = jnp.einsum("icgd,jcd->cgij", query_rows, keyed[:, :, 0]) * HD ** -0.5
    allowed = jnp.arange(ROWS)[None, :] <= jnp.arange(ROWS)[:, None]
    highest = jnp.max(jnp.where(allowed, scores, -jnp.inf), axis=-1, keepdims=True)
    weights = jnp.exp(jnp.where(allowed, scores - highest, -jnp.inf))
    totals = jnp.sum(weights, axis=-1)
    summed = jnp.einsum("cgij,jcd->icgd", weights.astype(jnp.bfloat16).astype(jnp.float32), keyed[:, :, 1])
    result = summed / jnp.transpose(totals, (2, 0, 1))[..., None]
    return result.astype(jnp.bfloat16).reshape(ROWS, HQ * HD)


def request_attention(request_queries, decode_kv, cache, cached_len, prefill_kv, page_owner, page_slot):
    groups = HQ // COPIES
    copy_head = (jnp.arange(COPIES) * KVH) // COPIES
    pages = prefill_kv.reshape(NPAGE, PAGE, KVH, 2 * HD)[:, :, copy_head]
    filled = cache.reshape(N_CTX, ROWS_DEV, REQ_PAGES, PAGE, COPIES, 2 * HD)
    filled = filled.at[page_owner, page_slot // HALF_PAGES, page_slot % HALF_PAGES].set(pages)
    filled = filled.reshape(ROWS // 16, 16, CL, COPIES, 2, HD)
    query_rows = request_queries.reshape(ROWS // 16, 16, COPIES, groups, HD)
    own_rows = decode_kv.reshape(ROWS, KVH, 2, HD)[:, copy_head].reshape(ROWS // 16, 16, COPIES, 2, HD)
    lengths = cached_len.reshape(ROWS // 16, 16)

    def one_block(items):
        block_cache, block_query, block_own, block_len = items
        cached = block_cache.astype(jnp.float32)
        query_f = block_query.astype(jnp.float32)
        own_f = block_own.astype(jnp.float32)
        scores = jnp.einsum("icgd,itcd->icgt", query_f, cached[:, :, :, 0]) * HD ** -0.5
        fresh = jnp.einsum("icgd,icd->icg", query_f, own_f[:, :, 0]) * HD ** -0.5
        allowed = (jnp.arange(CL)[None, :] < block_len[:, None])[:, None, None, :]
        highest = jnp.maximum(jnp.max(jnp.where(allowed, scores, -jnp.inf), axis=-1), fresh)
        weights = jnp.exp(jnp.where(allowed, scores - highest[..., None], -jnp.inf))
        fresh_weight = jnp.exp(fresh - highest)
        totals = jnp.sum(weights, axis=-1) + fresh_weight
        summed = jnp.einsum("icgt,itcd->icgd", weights.astype(jnp.bfloat16).astype(jnp.float32), cached[:, :, :, 1])
        summed = summed + fresh_weight.astype(jnp.bfloat16).astype(jnp.float32)[..., None] * own_f[:, :, None, 1]
        return (summed / totals[..., None]).astype(jnp.bfloat16).reshape(16, HQ * HD)

    return lax.map(one_block, (filled, query_rows, own_rows, lengths)).reshape(ROWS, HQ * HD)


def reference(hidden, queries, kv_weight, out_weight, cache, page_owner, page_slot, cached_len):
    prefill_kv, decode_kv = project_parts(hidden, kv_weight)
    span_attn = span_attention(queries[0], prefill_kv)
    request_attn = request_attention(queries[1], decode_kv, cache, cached_len, prefill_kv, page_owner, page_slot)
    first_out = jnp.dot(span_attn, out_weight, preferred_element_type=jnp.float32).astype(jnp.bfloat16)
    second_out = jnp.dot(request_attn, out_weight, preferred_element_type=jnp.float32).astype(jnp.bfloat16)
    return jnp.stack([first_out, second_out])
```

```python
import jax
import jax.numpy as jnp
from jax import lax
from jax.experimental import pallas as pl
from jax.experimental.pallas import tpu as pltpu
from jax.sharding import PartitionSpec as P

HD = 128
PAGE = 8
SIDE = 4
RANKS = 16
NCTX = 8
ROWS = 128
WIDE = 512
BLOCK = 16
SCALE = HD ** -0.5
NEG = -1e30
VMEM = pl.BlockSpec(memory_space=pltpu.VMEM)
SMEM = pl.BlockSpec(memory_space=pltpu.SMEM)
ANY = pl.BlockSpec(memory_space=pl.ANY)
F32 = jnp.float32
BF16 = jnp.bfloat16


def rank_of(group, a, b):
    return SIDE * a + b if group == 0 else SIDE * b + a


def tp_route(step_a, step_b):
    route = []
    for group in range(2):
        for a in range(SIDE):
            for b in range(SIDE):
                to = rank_of(group, (a + step_a) % SIDE, (b + step_b) % SIDE)
                route.append((group * RANKS + rank_of(group, a, b), group * RANKS + to))
    return route


def shift(block, step_a, step_b):
    return lax.ppermute(block, ("group", "tp"), tp_route(step_a, step_b))


def routed(block, groups, target):
    route = []
    for group in groups:
        for c in range(NCTX):
            for t in range(RANKS):
                g2, c2, t2 = target(group, c, t)
                route.append(((group * NCTX + c) * RANKS + t, (g2 * NCTX + c2) * RANKS + t2))
    return lax.ppermute(block, ("group", "ctx", "tp"), route)


def chunk(info, a, b):
    a, b = lax.rem(a, SIDE), lax.rem(b, SIDE)
    return jnp.where(info[0] == 0, SIDE * a + b, SIDE * b + a)


def behind(info, k, j):
    return chunk(info, info[1] + SIDE - k, info[2] + SIDE - j)


def ahead(info, k, j):
    return chunk(info, info[1] + k, info[2] + j)


def nt(x, y):
    return lax.dot_general(x, y, (((1,), (1,)), ((), ())), preferred_element_type=F32)


def cache_kernel(info, q_ref, cache_ref, len_ref, req_ref, slot_ref, o_ref, m_ref, l_ref):
    @pl.when(info[0] == 1)
    def _():
        i = pl.program_id(0)
        rows = pl.ds(pl.multiple_of(i * BLOCK, BLOCK), BLOCK)
        q = q_ref[0, rows, :]
        q = jnp.concatenate([q[:, :HD], q[:, HD:]], axis=0)
        keys = cache_ref[:, :, :HD].reshape(BLOCK * HD, HD)
        values = cache_ref[:, :, HD:].reshape(BLOCK * HD, HD)
        wide = nt(keys, q).reshape(BLOCK, HD, 2 * BLOCK)
        shape = (BLOCK, HD, 2 * BLOCK)
        own = lax.broadcasted_iota(jnp.int32, shape, 0) == lax.rem(
            lax.broadcasted_iota(jnp.int32, shape, 2), BLOCK
        )
        scores = jnp.sum(jnp.where(own, wide, 0.0), axis=0).T * SCALE
        row_hit = (
            lax.broadcasted_iota(jnp.int32, (BLOCK, HD), 0) + i * BLOCK == req_ref[...]
        ).astype(BF16)
        col_hit = (
            lax.broadcasted_iota(jnp.int32, (HD, HD), 0) // PAGE == slot_ref[...]
        ).astype(BF16)
        filled = nt(row_hit, col_hit)
        position = lax.broadcasted_iota(jnp.int32, (BLOCK, HD), 1)
        open_ = jnp.where((position < len_ref[...]) & (filled < 0.5), 1.0, 0.0)
        allowed = jnp.concatenate([open_, open_], axis=0) > 0.5
        scores = jnp.where(allowed, scores, NEG)
        top = jnp.max(scores, axis=1, keepdims=True)
        weights = jnp.where(allowed, jnp.exp(scores - top), 0.0)
        total = jnp.sum(weights, axis=1, keepdims=True)
        spread = jnp.concatenate([weights] * BLOCK, axis=1)
        shape = (2 * BLOCK, BLOCK * HD)
        own = (
            lax.rem(lax.broadcasted_iota(jnp.int32, shape, 0), BLOCK)
            == lax.broadcasted_iota(jnp.int32, shape, 1) // HD
        )
        spread = jnp.where(own, spread, 0.0).astype(BF16)
        summed = jnp.dot(spread, values, preferred_element_type=F32)
        for h in range(2):
            part = slice(h * BLOCK, (h + 1) * BLOCK)
            o_ref[h] = summed[part]
            m_ref[h] = jnp.broadcast_to(top[part], (BLOCK, HD))
            l_ref[h] = jnp.broadcast_to(total[part], (BLOCK, HD))


def cache_attention(info, queries, cache, lens, req, slot):
    steps = ROWS // BLOCK
    whole = lambda *shape: pl.BlockSpec(shape, lambda i, info: (0,) * len(shape))
    out = pl.BlockSpec((2, BLOCK, HD), lambda i, info: (0, i, 0))
    return pl.pallas_call(
        cache_kernel,
        grid_spec=pltpu.PrefetchScalarGridSpec(
            num_scalar_prefetch=1,
            grid=(steps,),
            in_specs=[
                whole(1, ROWS, 2 * HD),
                pl.BlockSpec((BLOCK, HD, 2 * HD), lambda i, info: (i * info[0], 0, 0)),
                pl.BlockSpec((BLOCK, HD), lambda i, info: (i, 0)),
                whole(1, HD),
                whole(1, HD),
            ],
            out_specs=[out] * 3,
        ),
        out_shape=[jax.ShapeDtypeStruct((2, ROWS, HD), F32)] * 3,
        compiler_params=pltpu.CompilerParams(vmem_limit_bytes=16 << 20),
        cost_estimate=pl.CostEstimate(
            flops=2_000_000_000, bytes_accessed=9 << 20, transcendentals=1 << 16
        ),
        name="cache_attention",
    )(info, queries, cache, lens, req, slot)


def project_first(info, held_ref, w_ref, acc_ref):
    total = jnp.zeros((ROWS, HD), F32)
    for j in range(SIDE):
        start = pl.multiple_of(behind(info, 0, j) * WIDE, WIDE)
        total += jnp.dot(held_ref[j], w_ref[pl.ds(start, WIDE), :], preferred_element_type=F32)
    acc_ref[...] = total


def project_rest(info, acc_ref, r1_ref, r2_ref, r3_ref, w_ref, kv_ref):
    total = acc_ref[...]
    for k, ref in ((1, r1_ref), (2, r2_ref), (3, r3_ref)):
        for j in range(SIDE):
            start = pl.multiple_of(behind(info, k, j) * WIDE, WIDE)
            total += jnp.dot(ref[j], w_ref[pl.ds(start, WIDE), :], preferred_element_type=F32)
    kv_ref[...] = total.astype(BF16)


def pair_kernel(info, own_ref, partner_ref, near_ref, cross_ref, x_ref):
    @pl.when(info[4] == 0)
    def _():
        x_ref[0] = own_ref[...]
        x_ref[1] = partner_ref[...]
        x_ref[2] = near_ref[...]
        x_ref[3] = cross_ref[...]

    @pl.when(info[4] == 1)
    def _():
        x_ref[0] = partner_ref[...]
        x_ref[1] = own_ref[...]
        x_ref[2] = cross_ref[...]
        x_ref[3] = near_ref[...]


def block_ctx(info, n):
    base = lax.rem(info[3] + NCTX - 2 * (n // 2), NCTX)
    return base if n % 2 == 0 else base + 1 - 2 * lax.rem(base, 2)


def span_kernel(info, q_ref, x0_ref, x1_ref, x2_ref, x3_ref, out_ref):
    @pl.when(info[0] == 0)
    def _():
        refs = (x0_ref, x1_ref, x2_ref, x3_ref)
        keys = [refs[n // 2][2 * (n % 2)] for n in range(NCTX)]
        values = [refs[n // 2][2 * (n % 2) + 1] for n in range(NCTX)]
        row = lax.broadcasted_iota(jnp.int32, (ROWS, HD), 0)
        col = lax.broadcasted_iota(jnp.int32, (ROWS, HD), 1)
        offset = row - col
        limits = [(block_ctx(info, n) - info[3]) * ROWS for n in range(NCTX)]
        for h in range(2):
            q = q_ref[0, :, h * HD : (h + 1) * HD]
            scores = [
                jnp.where(offset >= limits[n], nt(q, keys[n]) * SCALE, NEG)
                for n in range(NCTX)
            ]
            top = scores[0]
            for s in scores[1:]:
                top = jnp.maximum(top, s)
            top = jnp.max(top, axis=1, keepdims=True)
            total = jnp.zeros((ROWS, HD), F32)
            summed = jnp.zeros((ROWS, HD), F32)
            for n in range(NCTX):
                w = jnp.where(offset >= limits[n], jnp.exp(scores[n] - top), 0.0)
                total += w
                summed += jnp.dot(w.astype(BF16), values[n], preferred_element_type=F32)
            total = jnp.sum(total, axis=1, keepdims=True)
            out_ref[:, h * HD : (h + 1) * HD] = (summed / total).astype(BF16)


def finish_kernel(
    info, q_ref, x_ref, span_ref, own_ref, len_ref, req_ref, pos_ref, o_ref, m_ref, l_ref, w_ref,
    s0_ref, s1_ref, s2_ref, s3_ref, att_ref,
):
    @pl.when(info[0] == 0)
    def _():
        att_ref[...] = x_ref[...]

    @pl.when(info[0] == 1)
    def _():
        row = lax.broadcasted_iota(jnp.int32, (ROWS, HD), 0)
        allowed = []
        for n in range(NCTX):
            at = pl.ds(block_ctx(info, n), 1)
            allowed.append((req_ref[at, :] == row) & (pos_ref[at, :] < len_ref[...]))
        key_new = own_ref[0].astype(F32)
        value_new = own_ref[1].astype(F32)
        for h in range(2):
            q = q_ref[0, :, h * HD : (h + 1) * HD]
            scores = [
                jnp.where(allowed[n], nt(q, span_ref[2 * n]) * SCALE, NEG) for n in range(NCTX)
            ]
            fresh = jnp.sum(q.astype(F32) * key_new, axis=1, keepdims=True) * SCALE
            top = scores[0]
            for s in scores[1:]:
                top = jnp.maximum(top, s)
            top = jnp.max(top, axis=1, keepdims=True)
            top = jnp.maximum(jnp.maximum(top, fresh), m_ref[h])
            old = jnp.exp(m_ref[h] - top)
            new = jnp.exp(fresh - top)
            total = jnp.zeros((ROWS, HD), F32)
            summed = o_ref[h] * old + new.astype(BF16).astype(F32) * value_new
            for n in range(NCTX):
                w = jnp.where(allowed[n], jnp.exp(scores[n] - top), 0.0)
                total += w
                summed += jnp.dot(
                    w.astype(BF16), span_ref[2 * n + 1], preferred_element_type=F32
                )
            total = jnp.sum(total, axis=1, keepdims=True) + l_ref[h] * old + new
            att_ref[:, h * HD : (h + 1) * HD] = (summed / total).astype(BF16)

    att = att_ref[...]
    for k, ref in ((1, s1_ref), (3, s3_ref), (2, s2_ref), (0, s0_ref)):
        for j in range(SIDE):
            start = pl.multiple_of(ahead(info, k, j) * WIDE, WIDE)
            part = jnp.dot(att, w_ref[:, pl.ds(start, WIDE)], preferred_element_type=F32)
            ref[j] = part.astype(ref.dtype)


def sum_sets(s0_ref, r1_ref, r2_ref, r3_ref, u0_ref, u1_ref, u2_ref, u3_ref):
    for j, ref in enumerate((u0_ref, u1_ref, u2_ref, u3_ref)):
        total = s0_ref[j] + r1_ref[j].astype(F32) + r2_ref[j].astype(F32) + r3_ref[j].astype(F32)
        ref[...] = total.astype(ref.dtype)


def sum_chunks(u0_ref, r1_ref, r2_ref, r3_ref, out_ref):
    total = u0_ref[...] + r1_ref[...].astype(F32) + r2_ref[...].astype(F32) + r3_ref[...].astype(F32)
    out_ref[...] = total.astype(BF16)


def place_kernel(info, t0_ref, t1_ref, t2_ref, t3_ref, out_ref, sems):
    copies = []
    for k, ref in enumerate((t0_ref, t1_ref, t2_ref, t3_ref)):
        for j in range(SIDE):
            start = pl.multiple_of(behind(info, k, j) * WIDE, WIDE)
            copies.append(
                pltpu.make_async_copy(
                    ref.at[j], out_ref.at[:, pl.ds(start, WIDE)], sems.at[k * SIDE + j]
                )
            )
    for copy in copies:
        copy.start()
    for copy in copies:
        copy.wait()


def call(kernel, outs, in_specs, out_specs, flops, *args, scratch=(), limit=24 << 20):
    size = sum(x.size * x.dtype.itemsize for x in args)
    return pl.pallas_call(
        kernel,
        out_shape=outs,
        in_specs=in_specs,
        out_specs=out_specs,
        scratch_shapes=list(scratch),
        compiler_params=pltpu.CompilerParams(vmem_limit_bytes=limit),
        cost_estimate=pl.CostEstimate(flops=flops, bytes_accessed=size, transcendentals=0),
        name=kernel.__name__,
    )(*args)


def body(hidden, queries, kv_weight, out_weight, cache, page_owner, page_slot, cached_len):
    group = lax.axis_index("group")
    ctx = lax.axis_index("ctx")
    rank = lax.axis_index("tp")
    high, low = rank // SIDE, rank % SIDE
    a = jnp.where(group == 0, high, low)
    b = jnp.where(group == 0, low, high)
    info = jnp.stack([group, a, b, ctx, rank % 2]).astype(jnp.int32)
    st = jax.ShapeDtypeStruct

    h = hidden[0]
    near = [h] + [shift(h, 0, k) for k in range(1, SIDE)]
    held = jnp.stack(near)

    lens = jnp.broadcast_to(cached_len[:, None], (ROWS, HD))
    mine = page_owner == ctx
    req = jnp.where(mine, page_slot // PAGE, -1)
    slot = page_slot % PAGE
    tied, held = lax.optimization_barrier((queries, held))
    old = cache_attention(info, tied, cache, lens, req[None], slot[None])
    req_tok = jnp.repeat(req, PAGE).reshape(NCTX, ROWS)
    pos_tok = (slot[:, None] * PAGE + jnp.arange(PAGE)[None, :]).reshape(NCTX, ROWS)

    arrived = [shift(held, k, 0) for k in range(1, SIDE)]
    acc = call(
        project_first, st((ROWS, HD), F32), [SMEM, VMEM, VMEM], VMEM, 70_000_000,
        info, held, kv_weight,
    )
    acc, old = lax.optimization_barrier((acc, old))
    kv = call(
        project_rest, st((ROWS, HD), BF16), [SMEM] + [VMEM] * 5, VMEM, 200_000_000,
        info, acc, *arrived, kv_weight,
    )

    partner = routed(kv, (0, 1), lambda g, c, t: (g, c, t ^ 1))
    beside = routed(kv, (0,), lambda g, c, t: (g, c ^ 1, t))
    cross = routed(kv, (0,), lambda g, c, t: (g, c ^ 1, t ^ 1))
    x0 = call(
        pair_kernel, st((4, ROWS, HD), BF16), [SMEM] + [VMEM] * 4, VMEM, 1000,
        info, kv, partner, beside, cross,
    )
    xs = [x0] + [routed(x0, (0,), lambda g, c, t, k=k: (g, (c + k) % NCTX, t)) for k in (2, 4, 6)]
    span = routed(jnp.concatenate(xs), (0,), lambda g, c, t: (1, c, t))
    att = call(
        span_kernel, st((ROWS, 2 * HD), BF16), [SMEM] + [VMEM] * 5, VMEM, 200_000_000,
        info, queries, *xs,
    )
    sets = call(
        finish_kernel,
        [st((SIDE, ROWS, WIDE), F32)] + [st((SIDE, ROWS, WIDE), BF16)] * 3,
        [SMEM] + [VMEM] * 11, [VMEM] * 4, 800_000_000,
        info, queries, att, span, x0, lens, req_tok, pos_tok, *old, out_weight,
        scratch=[pltpu.VMEM((ROWS, 2 * HD), BF16)],
    )

    got = [shift(sets[k], k, 0) for k in range(1, SIDE)]
    sums = call(
        sum_sets, [st((ROWS, WIDE), F32)] + [st((ROWS, WIDE), BF16)] * 3,
        [VMEM] * 4, [VMEM] * 4, 1_000_000, sets[0], *got,
    )
    got = [shift(sums[k], 0, k) for k in range(1, SIDE)]
    done = call(
        sum_chunks, st((ROWS, WIDE), BF16), [VMEM] * 4, VMEM, 1_000_000, sums[0], *got
    )
    line = jnp.stack([done] + [shift(done, 0, k) for k in range(1, SIDE)])
    lines = [line] + [shift(line, k, 0) for k in range(1, SIDE)]
    out = call(
        place_kernel, st((ROWS, RANKS * WIDE), BF16), [SMEM] + [VMEM] * 4, ANY, 1000,
        info, *lines, scratch=[pltpu.SemaphoreType.DMA((RANKS,))],
    )
    return out[None]


def solution(mesh):
    return jax.shard_map(
        body,
        mesh=mesh,
        in_specs=(
            P("group", "ctx", "tp"),
            P("group", "ctx", "tp"),
            P(None, "tp"),
            P("tp", None),
            P("ctx", None, "tp"),
            P(),
            P(),
            P("ctx"),
        ),
        out_specs=P("group", "ctx", None),
        check_vma=False,
    )
```

```python
import jax
import jax.numpy as jnp
from jax import lax
from jax.experimental import pallas as pl
from jax.experimental.pallas import tpu as pltpu
from jax.sharding import PartitionSpec as P

HD = 128
PAGE = 8
SIDE = 4
RANKS = 16
NCTX = 8
ROWS = 128
WIDE = 512
BLOCK = 16
HALF = 64
SCALE = HD ** -0.5
NEG = -1e30
VMEM = pl.BlockSpec(memory_space=pltpu.VMEM)
SMEM = pl.BlockSpec(memory_space=pltpu.SMEM)
HBM = pl.BlockSpec(memory_space=pltpu.HBM)
F32 = jnp.float32
BF16 = jnp.bfloat16


def rank_of(group, a, b):
    return SIDE * a + b if group == 0 else SIDE * b + a


def tp_route(step_a, step_b):
    route = []
    for group in range(2):
        for a in range(SIDE):
            for b in range(SIDE):
                to = rank_of(group, (a + step_a) % SIDE, (b + step_b) % SIDE)
                route.append((group * RANKS + rank_of(group, a, b), group * RANKS + to))
    return route


def shift(block, step_a, step_b):
    return lax.ppermute(block, ("group", "tp"), tp_route(step_a, step_b))


def routed(block, groups, target):
    route = []
    for group in groups:
        for c in range(NCTX):
            for t in range(RANKS):
                g2, c2, t2 = target(group, c, t)
                route.append(((group * NCTX + c) * RANKS + t, (g2 * NCTX + c2) * RANKS + t2))
    return lax.ppermute(block, ("group", "ctx", "tp"), route)


def chunk(info, a, b):
    a, b = lax.rem(a, SIDE), lax.rem(b, SIDE)
    return jnp.where(info[0] == 0, SIDE * a + b, SIDE * b + a)


def behind(info, k, j):
    return chunk(info, info[1] + SIDE - k, info[2] + SIDE - j)


def nt(x, y):
    return lax.dot_general(x, y, (((1,), (1,)), ((), ())), preferred_element_type=F32)


def relay(low, high, step):
    left_low = step(low, 1)
    right_high = step(high, -1)
    left_high = step(high, 1)
    right_low = step(low, -1)
    far_low = step(left_low, 1)
    far_high = step(right_high, -1)
    return left_low, left_high, right_low, right_high, far_low, far_high


def along_a(block, k):
    return shift(block, k, 0)


def along_b(block, k):
    return shift(block, 0, k)


def cache_kernel(
    info, q_ref, other_ref, cache_ref, len_ref, req_ref, slot_ref, out_ref, q_buf, buf, sems
):
    base = info[0] * HALF
    steps = HALF // BLOCK
    copies = [
        pltpu.make_async_copy(
            cache_ref.at[pl.ds(base + i * BLOCK, BLOCK)], buf.at[i], sems.at[i]
        )
        for i in range(steps)
    ]
    for copy in copies:
        copy.start()

    @pl.when(info[0] == 0)
    def _():
        q_buf[...] = other_ref[0, :HALF, :]

    @pl.when(info[0] == 1)
    def _():
        q_buf[...] = q_ref[0, HALF:, :]

    col_hit = (
        lax.broadcasted_iota(jnp.int32, (HD, HD), 0) // PAGE == slot_ref[...]
    ).astype(BF16)
    lens = len_ref[pl.ds(base, HALF), :]
    for i in range(steps):
        copies[i].wait()
        rows = slice(i * BLOCK, (i + 1) * BLOCK)
        q = q_buf[rows, :]
        q = jnp.concatenate([q[:, :HD], q[:, HD:]], axis=0)
        keys = buf[i, :, :, :HD].reshape(BLOCK * HD, HD)
        values = buf[i, :, :, HD:].reshape(BLOCK * HD, HD)
        wide = nt(keys, q).reshape(BLOCK, HD, 2 * BLOCK)
        shape = (BLOCK, HD, 2 * BLOCK)
        own = lax.broadcasted_iota(jnp.int32, shape, 0) == lax.rem(
            lax.broadcasted_iota(jnp.int32, shape, 2), BLOCK
        )
        scores = jnp.sum(jnp.where(own, wide, 0.0), axis=0).T * SCALE
        row_hit = (
            lax.broadcasted_iota(jnp.int32, (BLOCK, HD), 0) + base + i * BLOCK == req_ref[...]
        ).astype(BF16)
        filled = nt(row_hit, col_hit)
        position = lax.broadcasted_iota(jnp.int32, (BLOCK, HD), 1)
        open_ = jnp.where((position < lens[rows]) & (filled < 0.5), 1.0, 0.0)
        allowed = jnp.concatenate([open_, open_], axis=0) > 0.5
        scores = jnp.where(allowed, scores, NEG)
        top = jnp.max(scores, axis=1, keepdims=True)
        weights = jnp.where(allowed, jnp.exp(scores - top), 0.0)
        total = jnp.sum(weights, axis=1, keepdims=True)
        spread = jnp.concatenate([weights] * BLOCK, axis=1)
        shape = (2 * BLOCK, BLOCK * HD)
        own = (
            lax.rem(lax.broadcasted_iota(jnp.int32, shape, 0), BLOCK)
            == lax.broadcasted_iota(jnp.int32, shape, 1) // HD
        )
        spread = jnp.where(own, spread, 0.0).astype(BF16)
        summed = jnp.dot(spread, values, preferred_element_type=F32)
        lane = lax.broadcasted_iota(jnp.int32, (2 * BLOCK, HD), 1)
        stats = jnp.where(lane < HALF, top, total)
        for h in range(2):
            part = slice(h * BLOCK, (h + 1) * BLOCK)
            out_ref[0, h, rows, :] = summed[part]
            out_ref[1, h, rows, :] = stats[part]


def project_first(info, low_ref, high_ref, w_ref, acc_ref):
    total = jnp.zeros((ROWS, HD), F32)
    for j in range(SIDE):
        ref = (low_ref, high_ref)[j // 2]
        start = pl.multiple_of(behind(info, 0, j) * WIDE, WIDE)
        total += jnp.dot(ref[j % 2], w_ref[pl.ds(start, WIDE), :], preferred_element_type=F32)
    acc_ref[...] = total


def project_near(info, acc_ref, l0_ref, l1_ref, r0_ref, r1_ref, w_ref, out_ref):
    total = acc_ref[...]
    for k, refs in ((1, (l0_ref, l1_ref)), (3, (r0_ref, r1_ref))):
        for j in range(SIDE):
            start = pl.multiple_of(behind(info, k, j) * WIDE, WIDE)
            total += jnp.dot(
                refs[j // 2][j % 2], w_ref[pl.ds(start, WIDE), :], preferred_element_type=F32
            )
    out_ref[...] = total


def project_far(info, acc_ref, f0_ref, f1_ref, w_ref, kv_ref):
    total = acc_ref[...]
    for j in range(SIDE):
        ref = (f0_ref, f1_ref)[j // 2]
        start = pl.multiple_of(behind(info, 2, j) * WIDE, WIDE)
        total += jnp.dot(ref[j % 2], w_ref[pl.ds(start, WIDE), :], preferred_element_type=F32)
    kv_ref[...] = total.astype(BF16)


def pack_kernel(info, own_ref, pair_ref, swap_ref, cross_ref, span_ref, new_ref, half_ref):
    def put(ref, first, second):
        ref[0] = first[...]
        ref[1] = second[...]

    @pl.when(info[4] == 0)
    def _():
        put(new_ref, own_ref, pair_ref)

    @pl.when(info[4] == 1)
    def _():
        put(new_ref, pair_ref, own_ref)

    @pl.when(info[0] == 0)
    def _():
        span_ref[...] = new_ref[...]
        half_ref[...] = new_ref[0]

    @pl.when((info[0] == 1) & (info[4] == 0))
    def _():
        put(span_ref, swap_ref, cross_ref)
        half_ref[...] = cross_ref[...]

    @pl.when((info[0] == 1) & (info[4] == 1))
    def _():
        put(span_ref, cross_ref, swap_ref)
        half_ref[...] = swap_ref[...]


def attend(q, keys, values, allowed, start):
    scores = [jnp.where(m, nt(q, k[...]) * SCALE, NEG) for m, k in zip(allowed, keys)]
    top = scores[0]
    for s in scores[1:]:
        top = jnp.maximum(top, s)
    top = jnp.max(top, axis=1, keepdims=True)
    top, total, summed = start(top)
    sums = jnp.zeros((ROWS, HD), F32)
    for s, m, v in zip(scores, allowed, values):
        w = jnp.where(m, jnp.exp(s - top), 0.0)
        sums += w
        summed += jnp.dot(w.astype(BF16), v[...], preferred_element_type=F32)
    total += jnp.sum(sums, axis=1, keepdims=True)
    return (summed / total).astype(BF16)


def finish_kernel(
    info, q_ref, span_ref, new_ref, z1_ref, z2_ref, z3_ref, z4_ref, r1_ref, r2_ref, r3_ref, r4_ref,
    len_ref, req_ref, pos_ref, mine_ref, theirs_ref, w_ref,
    s0_ref, s1l_ref, s1h_ref, s2l_ref, s2h_ref, s3l_ref, s3h_ref, att_ref, w_buf, sems,
):
    order = [(k, j) for k in (2, 1, 3, 0) for j in range(SIDE)]
    copies = []
    for n, (k, j) in enumerate(order):
        start = pl.multiple_of(chunk(info, info[1] + k, j) * WIDE, WIDE)
        copies.append(
            pltpu.make_async_copy(w_ref.at[:, pl.ds(start, WIDE)], w_buf.at[n], sems.at[n])
        )
        copies[-1].start()
    row = lax.broadcasted_iota(jnp.int32, (ROWS, HD), 0)
    col = lax.broadcasted_iota(jnp.int32, (ROWS, HD), 1)
    ctx = info[3]
    near = [(z1_ref, r1_ref), (z2_ref, r2_ref), (z3_ref, r3_ref)]

    @pl.when(info[0] == 0)
    def _():
        places = [lax.rem(ctx + NCTX - k, NCTX) for k in range(5)]
        places += [lax.rem(ctx + k, NCTX) for k in range(1, 4)]
        refs = [span_ref] + [z for z, _ in near] + [None] + [r for _, r in near]
        keys = [z4_ref if r is None else r.at[0] for r in refs]
        values = [r4_ref if r is None else r.at[1] for r in refs]
        allowed = [row - col >= (p - ctx) * ROWS for p in places]
        zero = jnp.zeros((ROWS, HD), F32)
        for h in range(2):
            lanes = slice(h * HD, (h + 1) * HD)
            att_ref[:, lanes] = attend(
                q_ref[0, :, lanes], keys, values, allowed, lambda top: (top, 0.0, zero)
            )

    @pl.when(info[0] == 1)
    def _():
        places = [lax.rem(ctx + k, NCTX) for k in range(5)]
        places += [lax.rem(ctx + NCTX - k, NCTX) for k in range(1, 4)]
        refs = [span_ref] + [z for z, _ in near] + [None] + [r for _, r in near]
        keys = [r4_ref if r is None else r.at[0] for r in refs]
        values = [z4_ref if r is None else r.at[1] for r in refs]
        allowed = [
            (req_ref[pl.ds(p, 1), :] == row) & (pos_ref[pl.ds(p, 1), :] < len_ref[...])
            for p in places
        ]
        key_new = new_ref[0].astype(F32)
        value_new = new_ref[1].astype(F32)
        for h in range(2):
            lanes = slice(h * HD, (h + 1) * HD)
            q = q_ref[0, :, lanes]
            fresh = jnp.sum(q.astype(F32) * key_new, axis=1, keepdims=True) * SCALE
            summed = jnp.concatenate([theirs_ref[0, h], mine_ref[0, h]], axis=0)
            stats = jnp.concatenate([theirs_ref[1, h], mine_ref[1, h]], axis=0)
            highest, total = stats[:, :1], stats[:, HALF : HALF + 1]

            def start(top):
                top = jnp.maximum(jnp.maximum(top, fresh), highest)
                old = jnp.exp(highest - top)
                new = jnp.exp(fresh - top)
                rounded = new.astype(BF16).astype(F32)
                return top, total * old + new, summed * old + rounded * value_new

            att_ref[:, lanes] = attend(q, keys, values, allowed, start)

    att = att_ref[...]
    outs = {1: (s1l_ref, s1h_ref), 2: (s2l_ref, s2h_ref), 3: (s3l_ref, s3h_ref)}
    for n, (k, j) in enumerate(order):
        copies[n].wait()
        part = jnp.dot(att, w_buf[n], preferred_element_type=F32)
        if k == 0:
            s0_ref[j] = part
        else:
            outs[k][j // 2][j % 2] = part.astype(BF16)


def add_kernel(own_ref, got_ref, out_ref):
    out_ref[...] = (own_ref[...].astype(F32) + got_ref[...].astype(F32)).astype(BF16)


def fold_kernel(s0_ref, ll_ref, lh_ref, rl_ref, rh_ref, low_ref, high_ref):
    for n, (left, right, out) in enumerate(((ll_ref, rl_ref, low_ref), (lh_ref, rh_ref, high_ref))):
        total = s0_ref[2 * n : 2 * n + 2] + left[...].astype(F32) + right[...].astype(F32)
        out[...] = total.astype(BF16)


def line_kernel(
    low_ref, high_ref, ll_ref, lh_ref, rl_ref, rh_ref, fl_ref, fh_ref, out_low_ref, out_high_ref
):
    for own, far, left, right, out in (
        (low_ref, fl_ref, ll_ref, rl_ref, out_low_ref),
        (high_ref, fh_ref, lh_ref, rh_ref, out_high_ref),
    ):
        first = own[...].astype(F32) + far[...].astype(F32)
        second = left[...].astype(F32) + right[...].astype(F32)
        out[...] = (first + second).astype(BF16)


def place(info, sources, out_ref, sems):
    copies = []
    for k, low, high in sources:
        for j in range(SIDE):
            start = pl.multiple_of(chunk(info, info[1] + SIDE - k, j) * WIDE, WIDE)
            ref = (low, high)[j // 2].at[j % 2]
            copies.append(
                pltpu.make_async_copy(
                    ref, out_ref.at[:, pl.ds(start, WIDE)], sems.at[len(copies)]
                )
            )
            copies[-1].start()
    for copy in copies:
        copy.wait()


def place_near(info, tl_ref, th_ref, ll_ref, lh_ref, rl_ref, rh_ref, out_ref, sems):
    place(info, ((0, tl_ref, th_ref), (1, ll_ref, lh_ref), (3, rl_ref, rh_ref)), out_ref, sems)


def place_far(info, held_ref, fl_ref, fh_ref, out_ref, sems):
    place(info, ((2, fl_ref, fh_ref),), out_ref, sems)


def call(kernel, outs, in_specs, out_specs, flops, *args, scratch=(), limit=24 << 20, aliases=None):
    size = sum(x.size * x.dtype.itemsize for x in args)
    return pl.pallas_call(
        kernel,
        out_shape=outs,
        in_specs=in_specs,
        out_specs=out_specs,
        scratch_shapes=list(scratch),
        input_output_aliases=aliases or {},
        compiler_params=pltpu.CompilerParams(vmem_limit_bytes=limit),
        cost_estimate=pl.CostEstimate(flops=flops, bytes_accessed=size, transcendentals=0),
        name=kernel.__name__,
    )(*args)


def body(hidden, queries, kv_weight, out_weight, cache, page_owner, page_slot, cached_len):
    group = lax.axis_index("group")
    ctx = lax.axis_index("ctx")
    rank = lax.axis_index("tp")
    high, low = rank // SIDE, rank % SIDE
    a = jnp.where(group == 0, high, low)
    b = jnp.where(group == 0, low, high)
    info = jnp.stack([group, a, b, ctx, rank % 2]).astype(jnp.int32)
    st = jax.ShapeDtypeStruct
    dma = pltpu.SemaphoreType.DMA
    both = (0, 1)
    swap = lambda x: routed(x, both, lambda g, c, t: (1 - g, c, t))
    half = st((2, ROWS, WIDE), BF16)

    h = hidden[0]
    near = [h] + [shift(h, 0, k) for k in range(1, SIDE)]
    other_queries = swap(queries)
    held = (jnp.stack(near[:2]), jnp.stack(near[2:]))
    ll, lh, rl, rh, fl, fh = relay(*held, along_a)

    lens = jnp.broadcast_to(cached_len[:, None], (ROWS, HD))
    mine = page_owner == ctx
    req = jnp.where(mine, page_slot // PAGE, -1)
    slot = page_slot % PAGE
    req_tok = jnp.repeat(req, PAGE).reshape(NCTX, ROWS)
    pos_tok = (slot[:, None] * PAGE + jnp.arange(PAGE)[None, :]).reshape(NCTX, ROWS)

    acc = call(
        project_first, st((ROWS, HD), F32), [SMEM] + [VMEM] * 3, VMEM, 70_000_000,
        info, *held, kv_weight,
    )
    tied, ll, rh = lax.optimization_barrier((queries, ll, rh))
    old = call(
        cache_kernel, st((2, 2, HALF, HD), F32), [SMEM, VMEM, VMEM, HBM, VMEM, VMEM, VMEM], VMEM,
        1_000_000_000, info, tied, other_queries, cache, lens, req[None], slot[None],
        scratch=[
            pltpu.VMEM((HALF, 2 * HD), BF16),
            pltpu.VMEM((HALF // BLOCK, BLOCK, HD, 2 * HD), BF16),
            dma((HALF // BLOCK,)),
        ],
        limit=54 << 20,
    )
    acc = call(
        project_near, st((ROWS, HD), F32), [SMEM] + [VMEM] * 6, VMEM, 140_000_000,
        info, acc, ll, lh, rl, rh, kv_weight,
    )
    acc, old = lax.optimization_barrier((acc, old))
    other_old = swap(old)
    kv = call(
        project_far, st((ROWS, HD), BF16), [SMEM] + [VMEM] * 4, VMEM, 70_000_000,
        info, acc, fl, fh, kv_weight,
    )

    pair = routed(kv, both, lambda g, c, t: (g, c, t ^ 1))
    swapped = swap(kv)
    cross = routed(kv, both, lambda g, c, t: (1 - g, c, t ^ 1))
    span, new, part = call(
        pack_kernel, [st((2, ROWS, HD), BF16)] * 2 + [st((ROWS, HD), BF16)],
        [SMEM] + [VMEM] * 4, [VMEM] * 3, 1000, info, kv, pair, swapped, cross,
    )

    def along_z(block, k):
        return routed(
            block, both, lambda g, c, t: (g, (c + (k if g == 0 else NCTX - k)) % NCTX, t)
        )

    zs = [along_z(x, k) for k, x in ((1, span), (2, span), (3, span), (4, part))]
    rs = [swap(z) for z in zs]
    small = st((2, ROWS, WIDE), BF16)
    sets = call(
        finish_kernel, [st((SIDE, ROWS, WIDE), F32)] + [small] * 6,
        [SMEM] + [VMEM] * 16 + [HBM], [VMEM] * 7, 800_000_000,
        info, queries, span, new, *zs, *rs, lens, req_tok, pos_tok, old, other_old, out_weight,
        scratch=[
            pltpu.VMEM((ROWS, 2 * HD), BF16),
            pltpu.VMEM((RANKS, 2 * HD, WIDE), BF16),
            dma((RANKS,)),
        ],
    )
    s0, s1l, s1h, s2l, s2h, s3l, s3h = sets
    to_right = shift(s2l, 1, 0)
    to_left = shift(s2h, -1, 0)
    lh = shift(s1h, 1, 0)
    rl = shift(s3l, -1, 0)
    add = lambda x, y: call(add_kernel, small, [VMEM] * 2, VMEM, 1000, x, y)
    ll = shift(add(s1l, to_right), 1, 0)
    rh = shift(add(s3h, to_left), -1, 0)
    line = call(fold_kernel, [small] * 2, [VMEM] * 5, [VMEM] * 2, 1000, s0, ll, lh, rl, rh)
    line = call(
        line_kernel, [small] * 2, [VMEM] * 8, [VMEM] * 2, 1000, *line, *relay(*line, along_b)
    )
    ll, lh, rl, rh, fl, fh = relay(*line, along_a)
    whole = st((ROWS, RANKS * WIDE), BF16)
    out = call(
        place_near, whole, [SMEM] + [VMEM] * 6, HBM, 1000, info, *line, ll, lh, rl, rh,
        scratch=[dma((3 * SIDE,))],
    )
    out = call(
        place_far, whole, [SMEM, HBM, VMEM, VMEM], HBM, 1000, info, out, fl, fh,
        scratch=[dma((SIDE,))], aliases={1: 0},
    )
    return out[None]


def solution(mesh):
    return jax.shard_map(
        body,
        mesh=mesh,
        in_specs=(
            P("group", "ctx", "tp"),
            P("group", "ctx", "tp"),
            P(None, "tp"),
            P("tp", None),
            P("ctx", None, "tp"),
            P(),
            P(),
            P("ctx"),
        ),
        out_specs=P("group", "ctx", None),
        check_vma=False,
    )
```

```python
import jax
import jax.numpy as jnp
from jax import lax
from jax.experimental import pallas as pl
from jax.experimental.pallas import tpu as pltpu
from jax.sharding import PartitionSpec as P

HD = 128
PAGE = 8
SIDE = 4
RANKS = 16
NCTX = 8
ROWS = 128
WIDE = 512
QUARTER = 2048
BLOCK = 32
HALF = 64
SCALE = HD ** -0.5
NEG = -1e30
VMEM = pl.BlockSpec(memory_space=pltpu.VMEM)
SMEM = pl.BlockSpec(memory_space=pltpu.SMEM)
HBM = pl.BlockSpec(memory_space=pltpu.HBM)
F32 = jnp.float32
BF16 = jnp.bfloat16


def rank_of(group, a, b):
    return SIDE * a + b if group == 0 else SIDE * b + a


def tp_route(step_a, step_b):
    route = []
    for group in range(2):
        for a in range(SIDE):
            for b in range(SIDE):
                to = rank_of(group, (a + step_a) % SIDE, (b + step_b) % SIDE)
                route.append((group * RANKS + rank_of(group, a, b), group * RANKS + to))
    return route


def shift(block, step_a, step_b):
    return lax.ppermute(block, ("group", "tp"), tp_route(step_a, step_b))


def routed(block, groups, target):
    route = []
    for group in groups:
        for c in range(NCTX):
            for t in range(RANKS):
                g2, c2, t2 = target(group, c, t)
                route.append(((group * NCTX + c) * RANKS + t, (g2 * NCTX + c2) * RANKS + t2))
    return lax.ppermute(block, ("group", "ctx", "tp"), route)


def chunk(info, a, b):
    a, b = lax.rem(a, SIDE), lax.rem(b, SIDE)
    return jnp.where(info[0] == 0, SIDE * a + b, SIDE * b + a)


def behind(info, k, j):
    return chunk(info, info[1] + SIDE - k, info[2] + SIDE - j)


def nt(x, y):
    return lax.dot_general(x, y, (((1,), (1,)), ((), ())), preferred_element_type=F32)


def relay(low, high, step):
    left_low = step(low, 1)
    right_high = step(high, -1)
    left_high = step(high, 1)
    right_low = step(low, -1)
    far_low = step(left_low, 1)
    far_high = step(right_high, -1)
    return left_low, left_high, right_low, right_high, far_low, far_high


def along_a(block, k):
    return shift(block, k, 0)


def along_b(block, k):
    return shift(block, 0, k)


def cache_kernel(
    info, q_ref, other_ref, cache_ref, len_ref, req_ref, slot_ref, out_ref, q_buf, buf, sems
):
    base = info[0] * HALF
    steps = HALF // BLOCK

    def fetch(i):
        start = pl.multiple_of(base + i * BLOCK, BLOCK)
        return pltpu.make_async_copy(cache_ref.at[pl.ds(start, BLOCK)], buf.at[i], sems.at[i])

    for i in range(steps):
        fetch(i).start()

    @pl.when(info[0] == 0)
    def _():
        q_buf[...] = other_ref[0, :HALF, :]

    @pl.when(info[0] == 1)
    def _():
        q_buf[...] = q_ref[0, HALF:, :]

    col_hit = (
        lax.broadcasted_iota(jnp.int32, (HD, HD), 0) // PAGE == slot_ref[...]
    ).astype(BF16)
    row_of = lax.rem(lax.broadcasted_iota(jnp.int32, (2 * BLOCK, HD), 0), BLOCK)
    position = lax.broadcasted_iota(jnp.int32, (BLOCK, HD), 1)
    lane = lax.broadcasted_iota(jnp.int32, (2 * BLOCK, HD), 1)

    def step(i, carry):
        fetch(i).wait()
        rows = pl.ds(pl.multiple_of(i * BLOCK, BLOCK), BLOCK)
        q = q_buf[rows, :]
        q = jnp.concatenate([q[:, :HD], q[:, HD:]], axis=0)
        keys = buf[i, :, :, :HD].reshape(BLOCK * HD, HD)
        values = buf[i, :, :, HD:].reshape(BLOCK * HD, HD)
        wide = nt(q, keys)
        scores = wide[:, :HD]
        for r in range(1, BLOCK):
            scores = jnp.where(row_of == r, wide[:, r * HD : (r + 1) * HD], scores)
        scores = scores * SCALE
        row_hit = (
            lax.broadcasted_iota(jnp.int32, (BLOCK, HD), 0) + (base + i * BLOCK) == req_ref[...]
        ).astype(BF16)
        filled = nt(row_hit, col_hit)
        lens = len_ref[pl.ds(pl.multiple_of(base + i * BLOCK, BLOCK), BLOCK), :]
        open_ = jnp.where((position < lens) & (filled < 0.5), 1.0, 0.0)
        allowed = jnp.concatenate([open_, open_], axis=0) > 0.5
        scores = jnp.where(allowed, scores, NEG)
        top = jnp.max(scores, axis=1, keepdims=True)
        weights = jnp.where(allowed, jnp.exp(scores - top), 0.0)
        total = jnp.sum(weights, axis=1, keepdims=True)
        spread = jnp.concatenate(
            [jnp.where(row_of == r, weights, 0.0).astype(BF16) for r in range(BLOCK)], axis=1
        )
        summed = jnp.dot(spread, values, preferred_element_type=F32)
        stats = jnp.where(lane < HALF, top, total)
        for h in range(2):
            part = slice(h * BLOCK, (h + 1) * BLOCK)
            out_ref[0, h, rows, :] = summed[part]
            out_ref[1, h, rows, :] = stats[part]
        return carry

    lax.fori_loop(0, steps, step, 0)


def project_first(info, low_ref, high_ref, w_ref, acc_ref):
    total = jnp.zeros((ROWS, HD), F32)
    for j in range(SIDE):
        ref = (low_ref, high_ref)[j // 2]
        start = pl.multiple_of(behind(info, 0, j) * WIDE, WIDE)
        total += jnp.dot(ref[j % 2], w_ref[pl.ds(start, WIDE), :], preferred_element_type=F32)
    acc_ref[...] = total


def project_near(info, acc_ref, l0_ref, l1_ref, r0_ref, r1_ref, w_ref, out_ref):
    total = acc_ref[...]
    for k, refs in ((1, (l0_ref, l1_ref)), (3, (r0_ref, r1_ref))):
        for j in range(SIDE):
            start = pl.multiple_of(behind(info, k, j) * WIDE, WIDE)
            total += jnp.dot(
                refs[j // 2][j % 2], w_ref[pl.ds(start, WIDE), :], preferred_element_type=F32
            )
    out_ref[...] = total


def project_far(info, acc_ref, f0_ref, f1_ref, w_ref, kv_ref):
    total = acc_ref[...]
    for j in range(SIDE):
        ref = (f0_ref, f1_ref)[j // 2]
        start = pl.multiple_of(behind(info, 2, j) * WIDE, WIDE)
        total += jnp.dot(ref[j % 2], w_ref[pl.ds(start, WIDE), :], preferred_element_type=F32)
    kv_ref[...] = total.astype(BF16)


def pack_kernel(info, own_ref, pair_ref, swap_ref, cross_ref, span_ref, new_ref, half_ref):
    def put(ref, first, second):
        ref[0] = first[...]
        ref[1] = second[...]

    @pl.when(info[4] == 0)
    def _():
        put(new_ref, own_ref, pair_ref)

    @pl.when(info[4] == 1)
    def _():
        put(new_ref, pair_ref, own_ref)

    @pl.when(info[0] == 0)
    def _():
        span_ref[...] = new_ref[...]
        half_ref[...] = new_ref[0]

    @pl.when((info[0] == 1) & (info[4] == 0))
    def _():
        put(span_ref, swap_ref, cross_ref)
        half_ref[...] = cross_ref[...]

    @pl.when((info[0] == 1) & (info[4] == 1))
    def _():
        put(span_ref, cross_ref, swap_ref)
        half_ref[...] = swap_ref[...]


def attend(q, keys, values, allowed, start):
    scores = [jnp.where(m, nt(q, k[...]) * SCALE, NEG) for m, k in zip(allowed, keys)]
    top = scores[0]
    for s in scores[1:]:
        top = jnp.maximum(top, s)
    top = jnp.max(top, axis=1, keepdims=True)
    top, total, summed = start(top)
    sums = jnp.zeros((ROWS, HD), F32)
    for s, m, v in zip(scores, allowed, values):
        w = jnp.where(m, jnp.exp(s - top), 0.0)
        sums += w
        summed += jnp.dot(w.astype(BF16), v[...], preferred_element_type=F32)
    total += jnp.sum(sums, axis=1, keepdims=True)
    return (summed / total).astype(BF16)


def finish_kernel(
    info, q_ref, span_ref, new_ref, z1_ref, z2_ref, z3_ref, z4_ref, r1_ref, r2_ref, r3_ref, r4_ref,
    len_ref, req_ref, pos_ref, mine_ref, theirs_ref, att_ref,
):
    row = lax.broadcasted_iota(jnp.int32, (ROWS, HD), 0)
    col = lax.broadcasted_iota(jnp.int32, (ROWS, HD), 1)
    ctx = info[3]
    near = [(z1_ref, r1_ref), (z2_ref, r2_ref), (z3_ref, r3_ref)]

    @pl.when(info[0] == 0)
    def _():
        places = [lax.rem(ctx + NCTX - k, NCTX) for k in range(5)]
        places += [lax.rem(ctx + k, NCTX) for k in range(1, 4)]
        refs = [span_ref] + [z for z, _ in near] + [None] + [r for _, r in near]
        keys = [z4_ref if r is None else r.at[0] for r in refs]
        values = [r4_ref if r is None else r.at[1] for r in refs]
        allowed = [row - col >= (p - ctx) * ROWS for p in places]
        zero = jnp.zeros((ROWS, HD), F32)
        for h in range(2):
            lanes = slice(h * HD, (h + 1) * HD)
            att_ref[:, lanes] = attend(
                q_ref[0, :, lanes], keys, values, allowed, lambda top: (top, 0.0, zero)
            )

    @pl.when(info[0] == 1)
    def _():
        places = [lax.rem(ctx + k, NCTX) for k in range(5)]
        places += [lax.rem(ctx + NCTX - k, NCTX) for k in range(1, 4)]
        refs = [span_ref] + [z for z, _ in near] + [None] + [r for _, r in near]
        keys = [r4_ref if r is None else r.at[0] for r in refs]
        values = [z4_ref if r is None else r.at[1] for r in refs]
        allowed = [
            (req_ref[pl.ds(p, 1), :] == row) & (pos_ref[pl.ds(p, 1), :] < len_ref[...])
            for p in places
        ]
        key_new = new_ref[0].astype(F32)
        value_new = new_ref[1].astype(F32)
        for h in range(2):
            lanes = slice(h * HD, (h + 1) * HD)
            q = q_ref[0, :, lanes]
            fresh = jnp.sum(q.astype(F32) * key_new, axis=1, keepdims=True) * SCALE
            summed = jnp.concatenate([theirs_ref[0, h], mine_ref[0, h]], axis=0)
            stats = jnp.concatenate([theirs_ref[1, h], mine_ref[1, h]], axis=0)
            highest, total = stats[:, :1], stats[:, HALF : HALF + 1]

            def start(top):
                top = jnp.maximum(jnp.maximum(top, fresh), highest)
                old = jnp.exp(highest - top)
                new = jnp.exp(fresh - top)
                rounded = new.astype(BF16).astype(F32)
                return top, total * old + new, summed * old + rounded * value_new

            att_ref[:, lanes] = attend(q, keys, values, allowed, start)


def fetch_kernel(info, w_ref, w0_ref, w1_ref, w2_ref, w3_ref, sems):
    copies = []
    for k, ref in enumerate((w0_ref, w1_ref, w2_ref, w3_ref)):
        start = pl.multiple_of(lax.rem(info[2] + k, SIDE) * QUARTER, QUARTER)
        copies.append(pltpu.make_async_copy(w_ref.at[:, pl.ds(start, QUARTER)], ref, sems.at[k]))
        copies[-1].start()
    for copy in copies:
        copy.wait()


def output_first(att_ref, w_ref, out_ref):
    for n in range(SIDE):
        cols = slice(n * WIDE, (n + 1) * WIDE)
        out_ref[:, cols] = jnp.dot(att_ref[...], w_ref[:, cols], preferred_element_type=F32)


def output_rest(
    acc_ref, a1_ref, a2_ref, a3_ref, w1_ref, w2_ref, w3_ref, low_ref, high_ref
):
    for n in range(SIDE):
        cols = slice(n * WIDE, (n + 1) * WIDE)
        total = acc_ref[:, cols]
        for att, w in ((a1_ref, w1_ref), (a2_ref, w2_ref), (a3_ref, w3_ref)):
            total += jnp.dot(att[...], w[:, cols], preferred_element_type=F32)
        half = (low_ref, high_ref)[n // 2]
        half[:, (n % 2) * WIDE : (n % 2 + 1) * WIDE] = total.astype(BF16)


def line_kernel(
    low_ref, high_ref, ll_ref, lh_ref, rl_ref, rh_ref, fl_ref, fh_ref, out_low_ref, out_high_ref
):
    for own, far, left, right, out in (
        (low_ref, fl_ref, ll_ref, rl_ref, out_low_ref),
        (high_ref, fh_ref, lh_ref, rh_ref, out_high_ref),
    ):
        first = own[...].astype(F32) + far[...].astype(F32)
        second = left[...].astype(F32) + right[...].astype(F32)
        out[...] = (first + second).astype(BF16)


def place(info, sources, out_ref, sems):
    copies = []
    for k, low, high in sources:
        start = lax.rem(info[2] + SIDE - k, SIDE) * QUARTER
        for n, ref in enumerate((low, high)):
            cols = pl.ds(pl.multiple_of(start + n * QUARTER // 2, QUARTER // 2), QUARTER // 2)
            copies.append(
                pltpu.make_async_copy(ref, out_ref.at[:, cols], sems.at[len(copies)])
            )
            copies[-1].start()
    for copy in copies:
        copy.wait()


def place_near(info, tl_ref, th_ref, ll_ref, lh_ref, rl_ref, rh_ref, out_ref, sems):
    place(info, ((0, tl_ref, th_ref), (1, ll_ref, lh_ref), (3, rl_ref, rh_ref)), out_ref, sems)


def place_far(info, held_ref, fl_ref, fh_ref, out_ref, sems):
    place(info, ((2, fl_ref, fh_ref),), out_ref, sems)


def call(kernel, outs, in_specs, out_specs, flops, *args, scratch=(), limit=24 << 20, aliases=None):
    size = sum(x.size * x.dtype.itemsize for x in args)
    return pl.pallas_call(
        kernel,
        out_shape=outs,
        in_specs=in_specs,
        out_specs=out_specs,
        scratch_shapes=list(scratch),
        input_output_aliases=aliases or {},
        compiler_params=pltpu.CompilerParams(vmem_limit_bytes=limit),
        cost_estimate=pl.CostEstimate(flops=flops, bytes_accessed=size, transcendentals=0),
        name=kernel.__name__,
    )(*args)


def body(hidden, queries, kv_weight, out_weight, cache, page_owner, page_slot, cached_len):
    group = lax.axis_index("group")
    ctx = lax.axis_index("ctx")
    rank = lax.axis_index("tp")
    high, low = rank // SIDE, rank % SIDE
    a = jnp.where(group == 0, high, low)
    b = jnp.where(group == 0, low, high)
    info = jnp.stack([group, a, b, ctx, rank % 2]).astype(jnp.int32)
    st = jax.ShapeDtypeStruct
    dma = pltpu.SemaphoreType.DMA
    both = (0, 1)
    swap = lambda x: routed(x, both, lambda g, c, t: (1 - g, c, t))

    h = hidden[0]
    near = [h] + [shift(h, 0, k) for k in range(1, SIDE)]
    other_queries = swap(queries)
    held = (jnp.stack(near[:2]), jnp.stack(near[2:]))
    ll, lh, rl, rh, fl, fh = relay(*held, along_a)

    lens = jnp.broadcast_to(cached_len[:, None], (ROWS, HD))
    mine = page_owner == ctx
    req = jnp.where(mine, page_slot // PAGE, -1)
    slot = page_slot % PAGE
    req_tok = jnp.repeat(req, PAGE).reshape(NCTX, ROWS)
    pos_tok = (slot[:, None] * PAGE + jnp.arange(PAGE)[None, :]).reshape(NCTX, ROWS)

    acc = call(
        project_first, st((ROWS, HD), F32), [SMEM] + [VMEM] * 3, VMEM, 70_000_000,
        info, *held, kv_weight,
    )
    fetched = call(
        fetch_kernel, [st((2 * HD, QUARTER), BF16)] * 4, [SMEM, HBM], [VMEM] * 4, 1000,
        info, out_weight, scratch=[dma((4,))],
    )
    *fetched, ll, rh = lax.optimization_barrier((*fetched, ll, rh))
    weights = [shift(fetched[k], 0, k) for k in (1, 3)]
    acc = call(
        project_near, st((ROWS, HD), F32), [SMEM] + [VMEM] * 6, VMEM, 140_000_000,
        info, acc, ll, lh, rl, rh, kv_weight,
    )
    kv = call(
        project_far, st((ROWS, HD), BF16), [SMEM] + [VMEM] * 4, VMEM, 70_000_000,
        info, acc, fl, fh, kv_weight,
    )

    pair = routed(kv, both, lambda g, c, t: (g, c, t ^ 1))
    swapped = swap(kv)
    cross = routed(kv, both, lambda g, c, t: (1 - g, c, t ^ 1))
    span, new, part = call(
        pack_kernel, [st((2, ROWS, HD), BF16)] * 2 + [st((ROWS, HD), BF16)],
        [SMEM] + [VMEM] * 4, [VMEM] * 3, 1000, info, kv, pair, swapped, cross,
    )

    tied, part, far_weight, *weights = lax.optimization_barrier(
        (queries, part, fetched[2], *weights)
    )
    weights = [fetched[0], weights[0], shift(far_weight, 0, 2), weights[1]]
    old = call(
        cache_kernel, st((2, 2, HALF, HD), F32), [SMEM, VMEM, VMEM, HBM, VMEM, VMEM, VMEM], VMEM,
        1_000_000_000, info, tied, other_queries, cache, lens, req[None], slot[None],
        scratch=[
            pltpu.VMEM((HALF, 2 * HD), BF16),
            pltpu.VMEM((HALF // BLOCK, BLOCK, HD, 2 * HD), BF16),
            dma((HALF // BLOCK,)),
        ],
        limit=54 << 20,
    )
    other_old = swap(old)

    def along_z(block, k):
        return routed(
            block, both, lambda g, c, t: (g, (c + (k if g == 0 else NCTX - k)) % NCTX, t)
        )

    zs = [along_z(x, k) for k, x in ((1, span), (2, span), (3, span), (4, part))]
    rs = [swap(z) for z in zs]
    att = call(
        finish_kernel, st((ROWS, 2 * HD), BF16), [SMEM] + [VMEM] * 16, VMEM, 200_000_000,
        info, queries, span, new, *zs, *rs, lens, req_tok, pos_tok, old, other_old,
    )
    atts = [shift(att, 0, k) for k in range(1, SIDE)]
    small = st((ROWS, QUARTER // 2), BF16)
    total = call(
        output_first, st((ROWS, QUARTER), F32), [VMEM] * 2, VMEM, 130_000_000, att, weights[0]
    )
    line = call(
        output_rest, [small] * 2, [VMEM] * 7, [VMEM] * 2, 400_000_000, total, *atts, *weights[1:]
    )
    line = call(
        line_kernel, [small] * 2, [VMEM] * 8, [VMEM] * 2, 1000, *line, *relay(*line, along_a)
    )
    ll, lh, rl, rh, fl, fh = relay(*line, along_b)
    whole = st((ROWS, RANKS * WIDE), BF16)
    out = call(
        place_near, whole, [SMEM] + [VMEM] * 6, HBM, 1000, info, *line, ll, lh, rl, rh,
        scratch=[dma((6,))],
    )
    out = call(
        place_far, whole, [SMEM, HBM, VMEM, VMEM], HBM, 1000, info, out, fl, fh,
        scratch=[dma((2,))], aliases={1: 0},
    )
    return out[None]


def solution(mesh):
    return jax.shard_map(
        body,
        mesh=mesh,
        in_specs=(
            P("group", "ctx", "tp"),
            P("group", "ctx", "tp"),
            P(None, "tp"),
            P("tp", None),
            P("ctx", None, "tp"),
            P(),
            P(),
            P("ctx"),
        ),
        out_specs=P("group", "ctx", None),
        check_vma=False,
    )
```

```python
import jax
import jax.numpy as jnp
from jax import lax
from jax.experimental import pallas as pl
from jax.experimental.pallas import tpu as pltpu
from jax.sharding import PartitionSpec as P

HD = 128
PAGE = 8
SIDE = 4
RANKS = 16
NCTX = 8
ROWS = 128
WIDE = 512
BLOCK = 32
HALF = 64
SCALE = HD ** -0.5
NEG = -1e30
VMEM = pl.BlockSpec(memory_space=pltpu.VMEM)
SMEM = pl.BlockSpec(memory_space=pltpu.SMEM)
HBM = pl.BlockSpec(memory_space=pltpu.HBM)
F32 = jnp.float32
BF16 = jnp.bfloat16


def rank_of(group, a, b):
    return SIDE * a + b if group == 0 else SIDE * b + a


def tp_route(step_a, step_b):
    route = []
    for group in range(2):
        for a in range(SIDE):
            for b in range(SIDE):
                to = rank_of(group, (a + step_a) % SIDE, (b + step_b) % SIDE)
                route.append((group * RANKS + rank_of(group, a, b), group * RANKS + to))
    return route


def shift(block, step_a, step_b):
    return lax.ppermute(block, ("group", "tp"), tp_route(step_a, step_b))


def routed(block, groups, target):
    route = []
    for group in groups:
        for c in range(NCTX):
            for t in range(RANKS):
                g2, c2, t2 = target(group, c, t)
                route.append(((group * NCTX + c) * RANKS + t, (g2 * NCTX + c2) * RANKS + t2))
    return lax.ppermute(block, ("group", "ctx", "tp"), route)


def chunk(info, a, b):
    a, b = lax.rem(a, SIDE), lax.rem(b, SIDE)
    return jnp.where(info[0] == 0, SIDE * a + b, SIDE * b + a)


def behind(info, k, j):
    return chunk(info, info[1] + SIDE - k, info[2] + SIDE - j)


def nt(x, y):
    return lax.dot_general(x, y, (((1,), (1,)), ((), ())), preferred_element_type=F32)


def relay(low, high, step):
    left_low = step(low, 1)
    right_high = step(high, -1)
    left_high = step(high, 1)
    right_low = step(low, -1)
    far_low = step(left_low, 1)
    far_high = step(right_high, -1)
    return left_low, left_high, right_low, right_high, far_low, far_high


def along_a(block, k):
    return shift(block, k, 0)


def along_b(block, k):
    return shift(block, 0, k)


def lane_column(ref):
    return jnp.broadcast_to(ref[...].astype(F32), (HD, HD)).T


def cache_kernel(
    info, q_ref, other_ref, cache_ref, len_ref, owner_ref, slot_ref, out_ref, q_buf, open_buf, buf,
    sems,
):
    base = info[0] * HALF
    steps = HALF // BLOCK

    def fetch(i):
        start = pl.multiple_of(base + i * BLOCK, BLOCK)
        return pltpu.make_async_copy(cache_ref.at[pl.ds(start, BLOCK)], buf.at[i], sems.at[i])

    for i in range(steps):
        fetch(i).start()

    @pl.when(info[0] == 0)
    def _():
        q_buf[...] = other_ref[0, :HALF, :]

    @pl.when(info[0] == 1)
    def _():
        q_buf[...] = q_ref[0, HALF:, :]

    request = lax.broadcasted_iota(jnp.int32, (ROWS, HD), 0)
    column = lax.broadcasted_iota(jnp.int32, (ROWS, HD), 1)
    slot = slot_ref[...]
    row_hit = (owner_ref[...] == info[3]) & (slot // PAGE == request)
    col_hit = request // PAGE == lax.rem(slot, PAGE)
    filled = nt(row_hit.astype(BF16), col_hit.astype(BF16))
    inside = column.astype(F32) < lane_column(len_ref)
    open_buf[...] = jnp.where(inside & (filled < 0.5), 1.0, 0.0)

    shape = (BLOCK, HD, 2 * BLOCK)
    own_key = lax.broadcasted_iota(jnp.int32, shape, 0) == lax.rem(
        lax.broadcasted_iota(jnp.int32, shape, 2), BLOCK
    )
    row_of = lax.rem(lax.broadcasted_iota(jnp.int32, (2 * BLOCK, HD), 0), BLOCK)
    lane = lax.broadcasted_iota(jnp.int32, (2 * BLOCK, HD), 1)

    def step(i, carry):
        fetch(i).wait()
        rows = pl.ds(pl.multiple_of(i * BLOCK, BLOCK), BLOCK)
        q = q_buf[rows, :]
        q = jnp.concatenate([q[:, :HD], q[:, HD:]], axis=0)
        keys = buf[i, :, :, :HD].reshape(BLOCK * HD, HD)
        values = buf[i, :, :, HD:].reshape(BLOCK * HD, HD)
        wide = nt(keys, q).reshape(shape)
        scores = jnp.sum(jnp.where(own_key, wide, 0.0), axis=0).T * SCALE
        open_ = open_buf[pl.ds(pl.multiple_of(base + i * BLOCK, BLOCK), BLOCK), :]
        allowed = jnp.concatenate([open_, open_], axis=0) > 0.5
        scores = jnp.where(allowed, scores, NEG)
        top = jnp.max(scores, axis=1, keepdims=True)
        weights = jnp.where(allowed, jnp.exp(scores - top), 0.0)
        total = jnp.sum(weights, axis=1, keepdims=True)
        spread = jnp.concatenate(
            [jnp.where(row_of == r, weights, 0.0).astype(BF16) for r in range(BLOCK)], axis=1
        )
        summed = jnp.dot(spread, values, preferred_element_type=F32)
        stats = jnp.where(lane < HALF, top, total)
        for h in range(2):
            part = slice(h * BLOCK, (h + 1) * BLOCK)
            out_ref[0, h, rows, :] = summed[part]
            out_ref[1, h, rows, :] = stats[part]
        return carry

    lax.fori_loop(0, steps, step, 0)


def join_kernel(first_ref, second_ref, out_ref):
    out_ref[0] = first_ref[...]
    out_ref[1] = second_ref[...]


def project_first(info, low_ref, high_ref, w_ref, acc_ref):
    total = jnp.zeros((ROWS, HD), F32)
    for j in range(SIDE):
        ref = (low_ref, high_ref)[j // 2]
        start = pl.multiple_of(behind(info, 0, j) * WIDE, WIDE)
        total += jnp.dot(ref[j % 2], w_ref[pl.ds(start, WIDE), :], preferred_element_type=F32)
    acc_ref[...] = total


def project_near(info, acc_ref, l0_ref, l1_ref, r0_ref, r1_ref, w_ref, out_ref):
    total = acc_ref[...]
    for k, refs in ((1, (l0_ref, l1_ref)), (3, (r0_ref, r1_ref))):
        for j in range(SIDE):
            start = pl.multiple_of(behind(info, k, j) * WIDE, WIDE)
            total += jnp.dot(
                refs[j // 2][j % 2], w_ref[pl.ds(start, WIDE), :], preferred_element_type=F32
            )
    out_ref[...] = total


def project_far(info, acc_ref, f0_ref, f1_ref, w_ref, kv_ref):
    total = acc_ref[...]
    for j in range(SIDE):
        ref = (f0_ref, f1_ref)[j // 2]
        start = pl.multiple_of(behind(info, 2, j) * WIDE, WIDE)
        total += jnp.dot(ref[j % 2], w_ref[pl.ds(start, WIDE), :], preferred_element_type=F32)
    kv_ref[...] = total.astype(BF16)


def pack_kernel(info, own_ref, pair_ref, swap_ref, cross_ref, span_ref, new_ref, half_ref):
    def put(ref, first, second):
        ref[0] = first[...]
        ref[1] = second[...]

    @pl.when(info[4] == 0)
    def _():
        put(new_ref, own_ref, pair_ref)

    @pl.when(info[4] == 1)
    def _():
        put(new_ref, pair_ref, own_ref)

    @pl.when(info[0] == 0)
    def _():
        span_ref[...] = new_ref[...]
        half_ref[...] = new_ref[0]

    @pl.when((info[0] == 1) & (info[4] == 0))
    def _():
        put(span_ref, swap_ref, cross_ref)
        half_ref[...] = cross_ref[...]

    @pl.when((info[0] == 1) & (info[4] == 1))
    def _():
        put(span_ref, cross_ref, swap_ref)
        half_ref[...] = swap_ref[...]


def attend(q, keys, values, allowed, start):
    scores = [jnp.where(m, nt(q, k[...]) * SCALE, NEG) for m, k in zip(allowed, keys)]
    top = scores[0]
    for s in scores[1:]:
        top = jnp.maximum(top, s)
    top = jnp.max(top, axis=1, keepdims=True)
    top, total, summed = start(top)
    sums = jnp.zeros((ROWS, HD), F32)
    for s, m, v in zip(scores, allowed, values):
        w = jnp.where(m, jnp.exp(s - top), 0.0)
        sums += w
        summed += jnp.dot(w.astype(BF16), v[...], preferred_element_type=F32)
    total += jnp.sum(sums, axis=1, keepdims=True)
    return (summed / total).astype(BF16)


def finish_kernel(
    info, q_ref, span_ref, new_ref, z1_ref, z2_ref, z3_ref, z4_ref, r1_ref, r2_ref, r3_ref, r4_ref,
    len_ref, owner_ref, slot_ref, mine_ref, theirs_ref, w_ref,
    s0_ref, s1l_ref, s1h_ref, s2l_ref, s2h_ref, s3l_ref, s3h_ref, att_ref,
):
    row = lax.broadcasted_iota(jnp.int32, (ROWS, HD), 0)
    col = lax.broadcasted_iota(jnp.int32, (ROWS, HD), 1)
    ctx = info[3]
    near = [(z1_ref, r1_ref), (z2_ref, r2_ref), (z3_ref, r3_ref)]

    @pl.when(info[0] == 0)
    def _():
        places = [lax.rem(ctx + NCTX - k, NCTX) for k in range(5)]
        places += [lax.rem(ctx + k, NCTX) for k in range(1, 4)]
        refs = [span_ref] + [z for z, _ in near] + [None] + [r for _, r in near]
        keys = [z4_ref if r is None else r.at[0] for r in refs]
        values = [r4_ref if r is None else r.at[1] for r in refs]
        allowed = [row - col >= (p - ctx) * ROWS for p in places]
        zero = jnp.zeros((ROWS, HD), F32)
        for h in range(2):
            lanes = slice(h * HD, (h + 1) * HD)
            att_ref[:, lanes] = attend(
                q_ref[0, :, lanes], keys, values, allowed, lambda top: (top, 0.0, zero)
            )

    @pl.when(info[0] == 1)
    def _():
        places = [lax.rem(ctx + k, NCTX) for k in range(5)]
        places += [lax.rem(ctx + NCTX - k, NCTX) for k in range(1, 4)]
        refs = [span_ref] + [z for z, _ in near] + [None] + [r for _, r in near]
        keys = [r4_ref if r is None else r.at[0] for r in refs]
        values = [z4_ref if r is None else r.at[1] for r in refs]
        slot = slot_ref[...]
        request = jnp.where(owner_ref[...] == ctx, slot // PAGE, -1).astype(F32)
        page = lax.rem(slot, PAGE).astype(F32)
        in_page = (lax.rem(row, 2 * PAGE) == col // PAGE).astype(BF16)
        lens = lane_column(len_ref)
        pages = lax.broadcasted_iota(jnp.int32, (1, HD), 1) // (2 * PAGE)
        allowed = []
        for p in places:
            picked = jnp.concatenate([request, page] * 8, axis=0)
            picked = jnp.where(pages == p, picked, 0.0).astype(BF16)
            token = jnp.dot(picked, in_page, preferred_element_type=F32)
            position = token[1:2] * PAGE + lax.rem(col[:1], PAGE).astype(F32)
            allowed.append((token[:1] == row.astype(F32)) & (position < lens))
        key_new = new_ref[0].astype(F32)
        value_new = new_ref[1].astype(F32)
        for h in range(2):
            lanes = slice(h * HD, (h + 1) * HD)
            q = q_ref[0, :, lanes]
            fresh = jnp.sum(q.astype(F32) * key_new, axis=1, keepdims=True) * SCALE
            summed = jnp.concatenate([theirs_ref[0, h], mine_ref[0, h]], axis=0)
            stats = jnp.concatenate([theirs_ref[1, h], mine_ref[1, h]], axis=0)
            highest, total = stats[:, :1], stats[:, HALF : HALF + 1]

            def start(top):
                top = jnp.maximum(jnp.maximum(top, fresh), highest)
                old = jnp.exp(highest - top)
                new = jnp.exp(fresh - top)
                rounded = new.astype(BF16).astype(F32)
                return top, total * old + new, summed * old + rounded * value_new

            att_ref[:, lanes] = attend(q, keys, values, allowed, start)

    att = att_ref[...]
    sets = {1: (s1l_ref, s1h_ref), 2: (s2l_ref, s2h_ref), 3: (s3l_ref, s3h_ref)}
    for k in (2, 1, 3, 0):
        for j in range(SIDE):
            start = pl.multiple_of(chunk(info, info[1] + k, j) * WIDE, WIDE)
            part = jnp.dot(att, w_ref[:, pl.ds(start, WIDE)], preferred_element_type=F32)
            if k == 0:
                s0_ref[j] = part
            else:
                sets[k][j // 2][j % 2] = part.astype(BF16)


def add_kernel(own_ref, got_ref, out_ref):
    out_ref[...] = (own_ref[...].astype(F32) + got_ref[...].astype(F32)).astype(BF16)


def fold_kernel(s0_ref, ll_ref, lh_ref, rl_ref, rh_ref, low_ref, high_ref):
    for n, (left, right, out) in enumerate(((ll_ref, rl_ref, low_ref), (lh_ref, rh_ref, high_ref))):
        total = s0_ref[2 * n : 2 * n + 2] + left[...].astype(F32) + right[...].astype(F32)
        out[...] = total.astype(BF16)


def line_kernel(
    low_ref, high_ref, ll_ref, lh_ref, rl_ref, rh_ref, fl_ref, fh_ref, out_low_ref, out_high_ref
):
    for own, far, left, right, out in (
        (low_ref, fl_ref, ll_ref, rl_ref, out_low_ref),
        (high_ref, fh_ref, lh_ref, rh_ref, out_high_ref),
    ):
        first = own[...].astype(F32) + far[...].astype(F32)
        second = left[...].astype(F32) + right[...].astype(F32)
        out[...] = (first + second).astype(BF16)


def place(info, sources, out_ref, sems):
    copies = []
    for k, low, high in sources:
        for j in range(SIDE):
            start = pl.multiple_of(chunk(info, info[1] + SIDE - k, j) * WIDE, WIDE)
            ref = (low, high)[j // 2].at[j % 2]
            copies.append(
                pltpu.make_async_copy(
                    ref, out_ref.at[:, pl.ds(start, WIDE)], sems.at[len(copies)]
                )
            )
            copies[-1].start()
    for copy in copies:
        copy.wait()


def place_near(info, tl_ref, th_ref, ll_ref, lh_ref, rl_ref, rh_ref, out_ref, sems):
    place(info, ((0, tl_ref, th_ref), (1, ll_ref, lh_ref), (3, rl_ref, rh_ref)), out_ref, sems)


def place_far(info, held_ref, fl_ref, fh_ref, out_ref, sems):
    place(info, ((2, fl_ref, fh_ref),), out_ref, sems)


def call(kernel, outs, in_specs, out_specs, flops, *args, scratch=(), limit=24 << 20, aliases=None):
    size = sum(x.size * x.dtype.itemsize for x in args)
    return pl.pallas_call(
        kernel,
        out_shape=outs,
        in_specs=in_specs,
        out_specs=out_specs,
        scratch_shapes=list(scratch),
        input_output_aliases=aliases or {},
        compiler_params=pltpu.CompilerParams(vmem_limit_bytes=limit),
        cost_estimate=pl.CostEstimate(flops=flops, bytes_accessed=size, transcendentals=0),
        name=kernel.__name__,
    )(*args)


def body(hidden, queries, kv_weight, out_weight, cache, page_owner, page_slot, cached_len):
    group = lax.axis_index("group")
    ctx = lax.axis_index("ctx")
    rank = lax.axis_index("tp")
    high, low = rank // SIDE, rank % SIDE
    a = jnp.where(group == 0, high, low)
    b = jnp.where(group == 0, low, high)
    info = jnp.stack([group, a, b, ctx, rank % 2]).astype(jnp.int32)
    st = jax.ShapeDtypeStruct
    dma = pltpu.SemaphoreType.DMA
    both = (0, 1)
    swap = lambda x: routed(x, both, lambda g, c, t: (1 - g, c, t))

    h = hidden[0]
    near = [h] + [shift(h, 0, k) for k in range(1, SIDE)]
    held = (
        call(join_kernel, st((2, ROWS, WIDE), BF16), [VMEM] * 2, VMEM, 1000, *near[:2]),
        jnp.stack(near[2:]),
    )
    ll, lh, rl, rh, fl, fh = relay(*held, along_a)
    owners, slots, lens = page_owner[None], page_slot[None], cached_len[None]

    acc = call(
        project_first, st((ROWS, HD), F32), [SMEM] + [VMEM] * 3, VMEM, 70_000_000,
        info, *held, kv_weight,
    )
    acc = call(
        project_near, st((ROWS, HD), F32), [SMEM] + [VMEM] * 6, VMEM, 140_000_000,
        info, acc, ll, lh, rl, rh, kv_weight,
    )
    kv = call(
        project_far, st((ROWS, HD), BF16), [SMEM] + [VMEM] * 4, VMEM, 70_000_000,
        info, acc, fl, fh, kv_weight,
    )

    kv, queries = lax.optimization_barrier((kv, queries))
    other_queries = swap(queries)
    pair = routed(kv, both, lambda g, c, t: (g, c, t ^ 1))
    swapped = swap(kv)
    cross = routed(kv, both, lambda g, c, t: (1 - g, c, t ^ 1))
    span, new, part = call(
        pack_kernel, [st((2, ROWS, HD), BF16)] * 2 + [st((ROWS, HD), BF16)],
        [SMEM] + [VMEM] * 4, [VMEM] * 3, 1000, info, kv, pair, swapped, cross,
    )

    def along_z(block, k):
        return routed(
            block, both, lambda g, c, t: (g, (c + (k if g == 0 else NCTX - k)) % NCTX, t)
        )

    zs = [along_z(x, k) for k, x in ((1, span), (2, span), (3, span), (4, part))]
    tied, zs[3] = lax.optimization_barrier((queries, zs[3]))
    old = call(
        cache_kernel, st((2, 2, HALF, HD), F32), [SMEM, VMEM, VMEM, HBM, VMEM, VMEM, VMEM], VMEM,
        1000, info, tied, other_queries, cache, lens, owners, slots,
        scratch=[
            pltpu.VMEM((HALF, 2 * HD), BF16),
            pltpu.VMEM((ROWS, HD), F32),
            pltpu.VMEM((HALF // BLOCK, BLOCK, HD, 2 * HD), BF16),
            dma((HALF // BLOCK,)),
        ],
        limit=51 << 20,
    )
    other_old = swap(old)

    rs = [swap(z) for z in zs]
    small = st((2, ROWS, WIDE), BF16)
    sets = call(
        finish_kernel, [st((SIDE, ROWS, WIDE), F32)] + [small] * 6,
        [SMEM] + [VMEM] * 17, [VMEM] * 7, 800_000_000,
        info, queries, span, new, *zs, *rs, lens, owners, slots, old, other_old, out_weight,
        scratch=[pltpu.VMEM((ROWS, 2 * HD), BF16)],
    )
    s0, s1l, s1h, s2l, s2h, s3l, s3h = sets
    to_right = shift(s2l, 1, 0)
    to_left = shift(s2h, -1, 0)
    lh = shift(s1h, 1, 0)
    rl = shift(s3l, -1, 0)
    add = lambda x, y: call(add_kernel, small, [VMEM] * 2, VMEM, 1000, x, y)
    ll = shift(add(s1l, to_right), 1, 0)
    rh = shift(add(s3h, to_left), -1, 0)
    line = call(fold_kernel, [small] * 2, [VMEM] * 5, [VMEM] * 2, 1000, s0, ll, lh, rl, rh)
    line = call(
        line_kernel, [small] * 2, [VMEM] * 8, [VMEM] * 2, 1000, *line, *relay(*line, along_b)
    )
    ll, lh, rl, rh, fl, fh = relay(*line, along_a)
    whole = st((ROWS, RANKS * WIDE), BF16)
    out = call(
        place_near, whole, [SMEM] + [VMEM] * 6, HBM, 1000, info, *line, ll, lh, rl, rh,
        scratch=[dma((3 * SIDE,))],
    )
    out = call(
        place_far, whole, [SMEM, HBM, VMEM, VMEM], HBM, 1000, info, out, fl, fh,
        scratch=[dma((SIDE,))], aliases={1: 0},
    )
    return out[None]


def solution(mesh):
    return jax.shard_map(
        body,
        mesh=mesh,
        in_specs=(
            P("group", "ctx", "tp"),
            P("group", "ctx", "tp"),
            P(None, "tp"),
            P("tp", None),
            P("ctx", None, "tp"),
            P(),
            P(),
            P("ctx"),
        ),
        out_specs=P("group", "ctx", None),
        check_vma=False,
    )
```

```python
import jax
import jax.numpy as jnp
from jax import lax
from jax.experimental import pallas as pl
from jax.experimental.pallas import tpu as pltpu
from jax.sharding import PartitionSpec as P

HD = 128
PAGE = 8
SIDE = 4
RANKS = 16
NCTX = 8
ROWS = 128
WIDE = 512
BLOCK = 32
HALF = 64
SCALE = HD ** -0.5
NEG = -1e30
VMEM = pl.BlockSpec(memory_space=pltpu.VMEM)
SMEM = pl.BlockSpec(memory_space=pltpu.SMEM)
HBM = pl.BlockSpec(memory_space=pltpu.HBM)
F32 = jnp.float32
BF16 = jnp.bfloat16


def rank_of(group, a, b):
    return SIDE * a + b if group == 0 else SIDE * b + a


def tp_route(step_a, step_b):
    route = []
    for group in range(2):
        for a in range(SIDE):
            for b in range(SIDE):
                to = rank_of(group, (a + step_a) % SIDE, (b + step_b) % SIDE)
                route.append((group * RANKS + rank_of(group, a, b), group * RANKS + to))
    return route


def shift(block, step_a, step_b):
    return lax.ppermute(block, ("group", "tp"), tp_route(step_a, step_b))


def routed(block, groups, target):
    route = []
    for group in groups:
        for c in range(NCTX):
            for t in range(RANKS):
                g2, c2, t2 = target(group, c, t)
                route.append(((group * NCTX + c) * RANKS + t, (g2 * NCTX + c2) * RANKS + t2))
    return lax.ppermute(block, ("group", "ctx", "tp"), route)


def chunk(info, a, b):
    a, b = lax.rem(a, SIDE), lax.rem(b, SIDE)
    return jnp.where(info[0] == 0, SIDE * a + b, SIDE * b + a)


def behind(info, k, j):
    return chunk(info, info[1] + SIDE - k, info[2] + SIDE - j)


def nt(x, y):
    return lax.dot_general(x, y, (((1,), (1,)), ((), ())), preferred_element_type=F32)


def relay(low, high, step):
    left_low = step(low, 1)
    right_high = step(high, -1)
    left_high = step(high, 1)
    right_low = step(low, -1)
    far_low = step(left_low, 1)
    far_high = step(right_high, -1)
    return left_low, left_high, right_low, right_high, far_low, far_high


def along_a(block, k):
    return shift(block, k, 0)


def along_b(block, k):
    return shift(block, 0, k)


def lane_column(ref):
    return jnp.broadcast_to(ref[...].astype(F32), (HD, HD)).T


def cache_kernel(
    info, q_ref, other_ref, cache_ref, len_ref, owner_ref, slot_ref, out_ref, q_buf, open_buf, buf,
    sems,
):
    base = info[0] * HALF
    steps = HALF // BLOCK

    def fetch(i):
        start = pl.multiple_of(base + i * BLOCK, BLOCK)
        return pltpu.make_async_copy(cache_ref.at[pl.ds(start, BLOCK)], buf.at[i], sems.at[i])

    for i in range(steps):
        fetch(i).start()

    @pl.when(info[0] == 0)
    def _():
        q_buf[...] = other_ref[0, :HALF, :]

    @pl.when(info[0] == 1)
    def _():
        q_buf[...] = q_ref[0, HALF:, :]

    request = lax.broadcasted_iota(jnp.int32, (ROWS, HD), 0)
    column = lax.broadcasted_iota(jnp.int32, (ROWS, HD), 1)
    slot = slot_ref[...]
    row_hit = (owner_ref[...] == info[3]) & (slot // PAGE == request)
    col_hit = request // PAGE == lax.rem(slot, PAGE)
    filled = nt(row_hit.astype(BF16), col_hit.astype(BF16))
    inside = column.astype(F32) < lane_column(len_ref)
    open_buf[...] = jnp.where(inside & (filled < 0.5), 1.0, 0.0)

    shape = (BLOCK, HD, 2 * BLOCK)
    own_key = lax.broadcasted_iota(jnp.int32, shape, 0) == lax.rem(
        lax.broadcasted_iota(jnp.int32, shape, 2), BLOCK
    )
    row_of = lax.rem(lax.broadcasted_iota(jnp.int32, (2 * BLOCK, HD), 0), BLOCK)
    lane = lax.broadcasted_iota(jnp.int32, (2 * BLOCK, HD), 1)

    def step(i, carry):
        fetch(i).wait()
        rows = pl.ds(pl.multiple_of(i * BLOCK, BLOCK), BLOCK)
        q = q_buf[rows, :]
        q = jnp.concatenate([q[:, :HD], q[:, HD:]], axis=0)
        keys = buf[i, :, :, :HD].reshape(BLOCK * HD, HD)
        values = buf[i, :, :, HD:].reshape(BLOCK * HD, HD)
        wide = nt(keys, q).reshape(shape)
        scores = jnp.sum(jnp.where(own_key, wide, 0.0), axis=0).T * SCALE
        open_ = open_buf[pl.ds(pl.multiple_of(base + i * BLOCK, BLOCK), BLOCK), :]
        allowed = jnp.concatenate([open_, open_], axis=0) > 0.5
        scores = jnp.where(allowed, scores, NEG)
        top = jnp.max(scores, axis=1, keepdims=True)
        weights = jnp.where(allowed, jnp.exp(scores - top), 0.0)
        total = jnp.sum(weights, axis=1, keepdims=True)
        spread = jnp.concatenate(
            [jnp.where(row_of == r, weights, 0.0).astype(BF16) for r in range(BLOCK)], axis=1
        )
        summed = jnp.dot(spread, values, preferred_element_type=F32)
        stats = jnp.where(lane < HALF, top, total)
        for h in range(2):
            part = slice(h * BLOCK, (h + 1) * BLOCK)
            out_ref[0, h, rows, :] = summed[part]
            out_ref[1, h, rows, :] = stats[part]
        return carry

    lax.fori_loop(0, steps, step, 0)


def join_kernel(first_ref, second_ref, out_ref):
    out_ref[0] = first_ref[...]
    out_ref[1] = second_ref[...]


def project_first(info, low_ref, high_ref, w_ref, acc_ref):
    total = jnp.zeros((ROWS, HD), F32)
    for j in range(SIDE):
        ref = (low_ref, high_ref)[j // 2]
        start = pl.multiple_of(behind(info, 0, j) * WIDE, WIDE)
        total += jnp.dot(ref[j % 2], w_ref[pl.ds(start, WIDE), :], preferred_element_type=F32)
    acc_ref[...] = total


def project_near(info, acc_ref, l0_ref, l1_ref, r0_ref, r1_ref, w_ref, out_ref):
    total = acc_ref[...]
    for k, refs in ((1, (l0_ref, l1_ref)), (3, (r0_ref, r1_ref))):
        for j in range(SIDE):
            start = pl.multiple_of(behind(info, k, j) * WIDE, WIDE)
            total += jnp.dot(
                refs[j // 2][j % 2], w_ref[pl.ds(start, WIDE), :], preferred_element_type=F32
            )
    out_ref[...] = total


def project_far(info, acc_ref, f0_ref, f1_ref, w_ref, kv_ref):
    total = acc_ref[...]
    for j in range(SIDE):
        ref = (f0_ref, f1_ref)[j // 2]
        start = pl.multiple_of(behind(info, 2, j) * WIDE, WIDE)
        total += jnp.dot(ref[j % 2], w_ref[pl.ds(start, WIDE), :], preferred_element_type=F32)
    kv_ref[...] = total.astype(BF16)


def pack_kernel(info, own_ref, pair_ref, swap_ref, cross_ref, span_ref, new_ref, half_ref):
    def put(ref, first, second):
        ref[0] = first[...]
        ref[1] = second[...]

    @pl.when(info[4] == 0)
    def _():
        put(new_ref, own_ref, pair_ref)

    @pl.when(info[4] == 1)
    def _():
        put(new_ref, pair_ref, own_ref)

    @pl.when(info[0] == 0)
    def _():
        span_ref[...] = new_ref[...]
        half_ref[...] = new_ref[0]

    @pl.when((info[0] == 1) & (info[4] == 0))
    def _():
        put(span_ref, swap_ref, cross_ref)
        half_ref[...] = cross_ref[...]

    @pl.when((info[0] == 1) & (info[4] == 1))
    def _():
        put(span_ref, cross_ref, swap_ref)
        half_ref[...] = swap_ref[...]


def attend(q, keys, values, allowed, start):
    scores = [jnp.where(m, nt(q, k[...]) * SCALE, NEG) for m, k in zip(allowed, keys)]
    top = scores[0]
    for s in scores[1:]:
        top = jnp.maximum(top, s)
    top = jnp.max(top, axis=1, keepdims=True)
    top, total, summed = start(top)
    sums = jnp.zeros((ROWS, HD), F32)
    for s, m, v in zip(scores, allowed, values):
        w = jnp.where(m, jnp.exp(s - top), 0.0)
        sums += w
        summed += jnp.dot(w.astype(BF16), v[...], preferred_element_type=F32)
    total += jnp.sum(sums, axis=1, keepdims=True)
    return (summed / total).astype(BF16)


def finish_kernel(
    info, q_ref, span_ref, new_ref, z1_ref, z2_ref, z3_ref, z4_ref, r1_ref, r2_ref, r3_ref, r4_ref,
    len_ref, owner_ref, slot_ref, mine_ref, theirs_ref, w_ref,
    s0_ref, s1l_ref, s1h_ref, s2l_ref, s2h_ref, s3l_ref, s3h_ref, att_ref,
):
    row = lax.broadcasted_iota(jnp.int32, (ROWS, HD), 0)
    col = lax.broadcasted_iota(jnp.int32, (ROWS, HD), 1)
    ctx = info[3]
    near = [(z1_ref, r1_ref), (z2_ref, r2_ref), (z3_ref, r3_ref)]

    @pl.when(info[0] == 0)
    def _():
        places = [lax.rem(ctx + NCTX - k, NCTX) for k in range(5)]
        places += [lax.rem(ctx + k, NCTX) for k in range(1, 4)]
        refs = [span_ref] + [z for z, _ in near] + [None] + [r for _, r in near]
        keys = [z4_ref if r is None else r.at[0] for r in refs]
        values = [r4_ref if r is None else r.at[1] for r in refs]
        allowed = [row - col >= (p - ctx) * ROWS for p in places]
        zero = jnp.zeros((ROWS, HD), F32)
        for h in range(2):
            lanes = slice(h * HD, (h + 1) * HD)
            att_ref[:, lanes] = attend(
                q_ref[0, :, lanes], keys, values, allowed, lambda top: (top, 0.0, zero)
            )

    @pl.when(info[0] == 1)
    def _():
        places = [lax.rem(ctx + k, NCTX) for k in range(5)]
        places += [lax.rem(ctx + NCTX - k, NCTX) for k in range(1, 4)]
        refs = [span_ref] + [z for z, _ in near] + [None] + [r for _, r in near]
        keys = [r4_ref if r is None else r.at[0] for r in refs]
        values = [z4_ref if r is None else r.at[1] for r in refs]
        slot = slot_ref[...]
        request = jnp.where(owner_ref[...] == ctx, slot // PAGE, -1).astype(F32)
        page = lax.rem(slot, PAGE).astype(F32)
        in_page = (lax.rem(row, 2 * PAGE) == col // PAGE).astype(BF16)
        lens = lane_column(len_ref)
        pages = lax.broadcasted_iota(jnp.int32, (1, HD), 1) // (2 * PAGE)
        allowed = []
        for p in places:
            picked = jnp.concatenate([request, page] * 8, axis=0)
            picked = jnp.where(pages == p, picked, 0.0).astype(BF16)
            token = jnp.dot(picked, in_page, preferred_element_type=F32)
            position = token[1:2] * PAGE + lax.rem(col[:1], PAGE).astype(F32)
            allowed.append((token[:1] == row.astype(F32)) & (position < lens))
        key_new = new_ref[0].astype(F32)
        value_new = new_ref[1].astype(F32)
        for h in range(2):
            lanes = slice(h * HD, (h + 1) * HD)
            q = q_ref[0, :, lanes]
            fresh = jnp.sum(q.astype(F32) * key_new, axis=1, keepdims=True) * SCALE
            summed = jnp.concatenate([theirs_ref[0, h], mine_ref[0, h]], axis=0)
            stats = jnp.concatenate([theirs_ref[1, h], mine_ref[1, h]], axis=0)
            highest, total = stats[:, :1], stats[:, HALF : HALF + 1]

            def start(top):
                top = jnp.maximum(jnp.maximum(top, fresh), highest)
                old = jnp.exp(highest - top)
                new = jnp.exp(fresh - top)
                rounded = new.astype(BF16).astype(F32)
                return top, total * old + new, summed * old + rounded * value_new

            att_ref[:, lanes] = attend(q, keys, values, allowed, start)

    att = att_ref[...]
    sets = {1: (s1l_ref, s1h_ref), 2: (s2l_ref, s2h_ref), 3: (s3l_ref, s3h_ref)}
    for k in (2, 1, 3, 0):
        for j in range(SIDE):
            start = pl.multiple_of(chunk(info, info[1] + k, j) * WIDE, WIDE)
            part = jnp.dot(att, w_ref[:, pl.ds(start, WIDE)], preferred_element_type=F32)
            if k == 0:
                s0_ref[j] = part
            else:
                sets[k][j // 2][j % 2] = part.astype(BF16)


def add_kernel(own_ref, got_ref, out_ref):
    out_ref[...] = (own_ref[...].astype(F32) + got_ref[...].astype(F32)).astype(BF16)


def fold_kernel(s0_ref, ll_ref, lh_ref, rl_ref, rh_ref, low_ref, high_ref):
    for n, (left, right, out) in enumerate(((ll_ref, rl_ref, low_ref), (lh_ref, rh_ref, high_ref))):
        total = s0_ref[2 * n : 2 * n + 2] + left[...].astype(F32) + right[...].astype(F32)
        out[...] = total.astype(BF16)


def line_kernel(
    low_ref, high_ref, ll_ref, lh_ref, rl_ref, rh_ref, fl_ref, fh_ref, out_low_ref, out_high_ref
):
    for own, far, left, right, out in (
        (low_ref, fl_ref, ll_ref, rl_ref, out_low_ref),
        (high_ref, fh_ref, lh_ref, rh_ref, out_high_ref),
    ):
        first = own[...].astype(F32) + far[...].astype(F32)
        second = left[...].astype(F32) + right[...].astype(F32)
        out[...] = (first + second).astype(BF16)


def place(info, sources, out_ref, sems):
    copies = []
    for k, low, high in sources:
        for j in range(SIDE):
            start = pl.multiple_of(chunk(info, info[1] + SIDE - k, j) * WIDE, WIDE)
            ref = (low, high)[j // 2].at[j % 2]
            copies.append(
                pltpu.make_async_copy(
                    ref, out_ref.at[:, pl.ds(start, WIDE)], sems.at[len(copies)]
                )
            )
            copies[-1].start()
    for copy in copies:
        copy.wait()


def place_near(info, tl_ref, th_ref, ll_ref, lh_ref, rl_ref, rh_ref, out_ref, sems):
    place(info, ((0, tl_ref, th_ref), (1, ll_ref, lh_ref), (3, rl_ref, rh_ref)), out_ref, sems)


def place_far(info, held_ref, fl_ref, fh_ref, out_ref, sems):
    place(info, ((2, fl_ref, fh_ref),), out_ref, sems)


def with_scalars(kernel):
    def wrapped(*refs):
        kernel([ref[0] for ref in refs[:5]], *refs[5:])

    wrapped.__name__ = kernel.__name__
    return wrapped


def call(kernel, outs, in_specs, out_specs, flops, *args, scratch=(), limit=24 << 20, aliases=None):
    if in_specs[0] is SMEM:
        kernel, in_specs, args = with_scalars(kernel), [SMEM] * 4 + in_specs, (*args[0], *args[1:])
        aliases = {n + 4: m for n, m in (aliases or {}).items()}
    size = sum(x.size * x.dtype.itemsize for x in args)
    return pl.pallas_call(
        kernel,
        out_shape=outs,
        in_specs=in_specs,
        out_specs=out_specs,
        scratch_shapes=list(scratch),
        input_output_aliases=aliases or {},
        compiler_params=pltpu.CompilerParams(vmem_limit_bytes=limit),
        cost_estimate=pl.CostEstimate(flops=flops, bytes_accessed=size, transcendentals=0),
        name=kernel.__name__,
    )(*args)


def body(hidden, queries, kv_weight, out_weight, cache, page_owner, page_slot, cached_len):
    group = lax.axis_index("group")
    ctx = lax.axis_index("ctx")
    rank = lax.axis_index("tp")
    high, low = rank // SIDE, rank % SIDE
    a = jnp.where(group == 0, high, low)
    b = jnp.where(group == 0, low, high)
    info = [x.astype(jnp.int32).reshape(1) for x in (group, a, b, ctx, rank % 2)]
    st = jax.ShapeDtypeStruct
    dma = pltpu.SemaphoreType.DMA
    both = (0, 1)
    swap = lambda x: routed(x, both, lambda g, c, t: (1 - g, c, t))

    h = hidden[0]
    near = [h] + [shift(h, 0, k) for k in range(1, SIDE)]
    held = (
        call(join_kernel, st((2, ROWS, WIDE), BF16), [VMEM] * 2, VMEM, 1000, *near[:2]),
        jnp.stack(near[2:]),
    )
    ll, lh, rl, rh, fl, fh = relay(*held, along_a)
    owners, slots, lens = page_owner[None], page_slot[None], cached_len[None]

    acc = call(
        project_first, st((ROWS, HD), F32), [SMEM] + [VMEM] * 3, VMEM, 70_000_000,
        info, *held, kv_weight,
    )
    acc = call(
        project_near, st((ROWS, HD), F32), [SMEM] + [VMEM] * 6, VMEM, 140_000_000,
        info, acc, ll, lh, rl, rh, kv_weight,
    )
    kv = call(
        project_far, st((ROWS, HD), BF16), [SMEM] + [VMEM] * 4, VMEM, 70_000_000,
        info, acc, fl, fh, kv_weight,
    )

    kv, queries = lax.optimization_barrier((kv, queries))
    other_queries = swap(queries)
    pair = routed(kv, both, lambda g, c, t: (g, c, t ^ 1))
    swapped = swap(kv)
    cross = routed(kv, both, lambda g, c, t: (1 - g, c, t ^ 1))
    span, new, part = call(
        pack_kernel, [st((2, ROWS, HD), BF16)] * 2 + [st((ROWS, HD), BF16)],
        [SMEM] + [VMEM] * 4, [VMEM] * 3, 1000, info, kv, pair, swapped, cross,
    )

    def along_z(block, k):
        return routed(
            block, both, lambda g, c, t: (g, (c + (k if g == 0 else NCTX - k)) % NCTX, t)
        )

    zs = [along_z(x, k) for k, x in ((1, span), (2, span), (3, span), (4, part))]
    tied, zs[3] = lax.optimization_barrier((queries, zs[3]))
    old = call(
        cache_kernel, st((2, 2, HALF, HD), F32), [SMEM, VMEM, VMEM, HBM, VMEM, VMEM, VMEM], VMEM,
        1000, info, tied, other_queries, cache, lens, owners, slots,
        scratch=[
            pltpu.VMEM((HALF, 2 * HD), BF16),
            pltpu.VMEM((ROWS, HD), F32),
            pltpu.VMEM((HALF // BLOCK, BLOCK, HD, 2 * HD), BF16),
            dma((HALF // BLOCK,)),
        ],
        limit=51 << 20,
    )
    other_old = swap(old)

    rs = [swap(z) for z in zs]
    small = st((2, ROWS, WIDE), BF16)
    sets = call(
        finish_kernel, [st((SIDE, ROWS, WIDE), F32)] + [small] * 6,
        [SMEM] + [VMEM] * 17, [VMEM] * 7, 800_000_000,
        info, queries, span, new, *zs, *rs, lens, owners, slots, old, other_old, out_weight,
        scratch=[pltpu.VMEM((ROWS, 2 * HD), BF16)],
    )
    s0, s1l, s1h, s2l, s2h, s3l, s3h = sets
    to_right = shift(s2l, 1, 0)
    to_left = shift(s2h, -1, 0)
    lh = shift(s1h, 1, 0)
    rl = shift(s3l, -1, 0)
    add = lambda x, y: call(add_kernel, small, [VMEM] * 2, VMEM, 1000, x, y)
    ll = shift(add(s1l, to_right), 1, 0)
    rh = shift(add(s3h, to_left), -1, 0)
    line = call(fold_kernel, [small] * 2, [VMEM] * 5, [VMEM] * 2, 1000, s0, ll, lh, rl, rh)
    line = call(
        line_kernel, [small] * 2, [VMEM] * 8, [VMEM] * 2, 1000, *line, *relay(*line, along_b)
    )
    ll, lh, rl, rh, fl, fh = relay(*line, along_a)
    whole = st((ROWS, RANKS * WIDE), BF16)
    out = call(
        place_near, whole, [SMEM] + [VMEM] * 6, HBM, 1000, info, *line, ll, lh, rl, rh,
        scratch=[dma((3 * SIDE,))],
    )
    out = call(
        place_far, whole, [SMEM, HBM, VMEM, VMEM], HBM, 1000, info, out, fl, fh,
        scratch=[dma((SIDE,))], aliases={1: 0},
    )
    return out[None]


def solution(mesh):
    return jax.shard_map(
        body,
        mesh=mesh,
        in_specs=(
            P("group", "ctx", "tp"),
            P("group", "ctx", "tp"),
            P(None, "tp"),
            P("tp", None),
            P("ctx", None, "tp"),
            P(),
            P(),
            P("ctx"),
        ),
        out_specs=P("group", "ctx", None),
        check_vma=False,
    )
```

```python
import jax
import jax.numpy as jnp
from jax import lax
from jax.experimental import pallas as pl
from jax.experimental.pallas import tpu as pltpu
from jax.sharding import PartitionSpec as P

HD = 128
PAGE = 8
SIDE = 4
RANKS = 16
NCTX = 8
ROWS = 128
WIDE = 512
BLOCK = 32
HALF = 64
SCALE = HD ** -0.5
NEG = -1e30
VMEM = pl.BlockSpec(memory_space=pltpu.VMEM)
SMEM = pl.BlockSpec(memory_space=pltpu.SMEM)
HBM = pl.BlockSpec(memory_space=pltpu.HBM)
F32 = jnp.float32
BF16 = jnp.bfloat16


def rank_of(group, a, b):
    return SIDE * a + b if group == 0 else SIDE * b + a


def tp_route(step_a, step_b):
    route = []
    for group in range(2):
        for a in range(SIDE):
            for b in range(SIDE):
                to = rank_of(group, (a + step_a) % SIDE, (b + step_b) % SIDE)
                route.append((group * RANKS + rank_of(group, a, b), group * RANKS + to))
    return route


def shift(block, step_a, step_b):
    return lax.ppermute(block, ("group", "tp"), tp_route(step_a, step_b))


def routed(block, groups, target):
    route = []
    for group in groups:
        for c in range(NCTX):
            for t in range(RANKS):
                g2, c2, t2 = target(group, c, t)
                route.append(((group * NCTX + c) * RANKS + t, (g2 * NCTX + c2) * RANKS + t2))
    return lax.ppermute(block, ("group", "ctx", "tp"), route)


def chunk(info, a, b):
    a, b = lax.rem(a, SIDE), lax.rem(b, SIDE)
    return jnp.where(info[0] == 0, SIDE * a + b, SIDE * b + a)


def behind(info, k, j):
    return chunk(info, info[1] + SIDE - k, info[2] + SIDE - j)


def nt(x, y):
    return lax.dot_general(x, y, (((1,), (1,)), ((), ())), preferred_element_type=F32)


def relay(low, high, step):
    left_low = step(low, 1)
    right_high = step(high, -1)
    left_high = step(high, 1)
    right_low = step(low, -1)
    far_low = step(left_low, 1)
    far_high = step(right_high, -1)
    return left_low, left_high, right_low, right_high, far_low, far_high


def along_a(block, k):
    return shift(block, k, 0)


def along_b(block, k):
    return shift(block, 0, k)


def lane_column(ref):
    return jnp.broadcast_to(ref[...].astype(F32), (HD, HD)).T


def cache_rows(info, order_ref, cache_ref, out_ref, sems):
    base = info[0] * HALF
    copies = []
    for i in range(HALF // BLOCK):
        start = pl.multiple_of(base + i * BLOCK, BLOCK)
        copies.append(
            pltpu.make_async_copy(cache_ref.at[pl.ds(start, BLOCK)], out_ref.at[i], sems.at[i])
        )
        copies[-1].start()
    for copy in copies:
        copy.wait()


def cache_kernel(
    info, q_ref, other_ref, buf, len_ref, owner_ref, slot_ref, out_ref, q_buf, open_buf
):
    base = info[0] * HALF
    steps = HALF // BLOCK

    @pl.when(info[0] == 0)
    def _():
        q_buf[...] = other_ref[0, :HALF, :]

    @pl.when(info[0] == 1)
    def _():
        q_buf[...] = q_ref[0, HALF:, :]

    request = lax.broadcasted_iota(jnp.int32, (ROWS, HD), 0)
    column = lax.broadcasted_iota(jnp.int32, (ROWS, HD), 1)
    slot = slot_ref[...]
    row_hit = (owner_ref[...] == info[3]) & (slot // PAGE == request)
    col_hit = request // PAGE == lax.rem(slot, PAGE)
    filled = nt(row_hit.astype(BF16), col_hit.astype(BF16))
    inside = column.astype(F32) < lane_column(len_ref)
    open_buf[...] = jnp.where(inside & (filled < 0.5), 1.0, 0.0)

    shape = (BLOCK, HD, 2 * BLOCK)
    own_key = lax.broadcasted_iota(jnp.int32, shape, 0) == lax.rem(
        lax.broadcasted_iota(jnp.int32, shape, 2), BLOCK
    )
    row_of = lax.rem(lax.broadcasted_iota(jnp.int32, (2 * BLOCK, HD), 0), BLOCK)
    lane = lax.broadcasted_iota(jnp.int32, (2 * BLOCK, HD), 1)

    def step(i, carry):
        rows = pl.ds(pl.multiple_of(i * BLOCK, BLOCK), BLOCK)
        q = q_buf[rows, :]
        q = jnp.concatenate([q[:, :HD], q[:, HD:]], axis=0)
        keys = buf[i, :, :, :HD].reshape(BLOCK * HD, HD)
        values = buf[i, :, :, HD:].reshape(BLOCK * HD, HD)
        wide = nt(keys, q).reshape(shape)
        scores = jnp.sum(jnp.where(own_key, wide, 0.0), axis=0).T * SCALE
        open_ = open_buf[pl.ds(pl.multiple_of(base + i * BLOCK, BLOCK), BLOCK), :]
        allowed = jnp.concatenate([open_, open_], axis=0) > 0.5
        scores = jnp.where(allowed, scores, NEG)
        top = jnp.max(scores, axis=1, keepdims=True)
        weights = jnp.where(allowed, jnp.exp(scores - top), 0.0)
        total = jnp.sum(weights, axis=1, keepdims=True)
        spread = jnp.concatenate(
            [jnp.where(row_of == r, weights, 0.0).astype(BF16) for r in range(BLOCK)], axis=1
        )
        summed = jnp.dot(spread, values, preferred_element_type=F32)
        stats = jnp.where(lane < HALF, top, total)
        for h in range(2):
            part = slice(h * BLOCK, (h + 1) * BLOCK)
            out_ref[0, h, rows, :] = summed[part]
            out_ref[1, h, rows, :] = stats[part]
        return carry

    lax.fori_loop(0, steps, step, 0)


def join_kernel(first_ref, second_ref, out_ref):
    out_ref[0] = first_ref[...]
    out_ref[1] = second_ref[...]


def project_first(info, low_ref, high_ref, w_ref, acc_ref):
    total = jnp.zeros((ROWS, HD), F32)
    for j in range(SIDE):
        ref = (low_ref, high_ref)[j // 2]
        start = pl.multiple_of(behind(info, 0, j) * WIDE, WIDE)
        total += jnp.dot(ref[j % 2], w_ref[pl.ds(start, WIDE), :], preferred_element_type=F32)
    acc_ref[...] = total


def project_near(info, acc_ref, l0_ref, l1_ref, r0_ref, r1_ref, w_ref, out_ref):
    total = acc_ref[...]
    for k, refs in ((1, (l0_ref, l1_ref)), (3, (r0_ref, r1_ref))):
        for j in range(SIDE):
            start = pl.multiple_of(behind(info, k, j) * WIDE, WIDE)
            total += jnp.dot(
                refs[j // 2][j % 2], w_ref[pl.ds(start, WIDE), :], preferred_element_type=F32
            )
    out_ref[...] = total


def project_far(info, acc_ref, f0_ref, f1_ref, w_ref, kv_ref):
    total = acc_ref[...]
    for j in range(SIDE):
        ref = (f0_ref, f1_ref)[j // 2]
        start = pl.multiple_of(behind(info, 2, j) * WIDE, WIDE)
        total += jnp.dot(ref[j % 2], w_ref[pl.ds(start, WIDE), :], preferred_element_type=F32)
    kv_ref[...] = total.astype(BF16)


def pack_kernel(info, own_ref, pair_ref, swap_ref, cross_ref, span_ref, new_ref, half_ref):
    def put(ref, first, second):
        ref[0] = first[...]
        ref[1] = second[...]

    @pl.when(info[4] == 0)
    def _():
        put(new_ref, own_ref, pair_ref)

    @pl.when(info[4] == 1)
    def _():
        put(new_ref, pair_ref, own_ref)

    @pl.when(info[0] == 0)
    def _():
        span_ref[...] = new_ref[...]
        half_ref[...] = new_ref[0]

    @pl.when((info[0] == 1) & (info[4] == 0))
    def _():
        put(span_ref, swap_ref, cross_ref)
        half_ref[...] = cross_ref[...]

    @pl.when((info[0] == 1) & (info[4] == 1))
    def _():
        put(span_ref, cross_ref, swap_ref)
        half_ref[...] = swap_ref[...]


def attend(q, keys, values, allowed, start):
    scores = [jnp.where(m, nt(q, k[...]) * SCALE, NEG) for m, k in zip(allowed, keys)]
    top = scores[0]
    for s in scores[1:]:
        top = jnp.maximum(top, s)
    top = jnp.max(top, axis=1, keepdims=True)
    top, total, summed = start(top)
    sums = jnp.zeros((ROWS, HD), F32)
    for s, m, v in zip(scores, allowed, values):
        w = jnp.where(m, jnp.exp(s - top), 0.0)
        sums += w
        summed += jnp.dot(w.astype(BF16), v[...], preferred_element_type=F32)
    total += jnp.sum(sums, axis=1, keepdims=True)
    return (summed / total).astype(BF16)


def finish_kernel(
    info, q_ref, span_ref, new_ref, z1_ref, z2_ref, z3_ref, z4_ref, r1_ref, r2_ref, r3_ref, r4_ref,
    len_ref, owner_ref, slot_ref, mine_ref, theirs_ref, w_ref,
    att_ref, s2l_ref, s2h_ref,
):
    row = lax.broadcasted_iota(jnp.int32, (ROWS, HD), 0)
    col = lax.broadcasted_iota(jnp.int32, (ROWS, HD), 1)
    ctx = info[3]
    near = [(z1_ref, r1_ref), (z2_ref, r2_ref), (z3_ref, r3_ref)]

    @pl.when(info[0] == 0)
    def _():
        places = [lax.rem(ctx + NCTX - k, NCTX) for k in range(5)]
        places += [lax.rem(ctx + k, NCTX) for k in range(1, 4)]
        refs = [span_ref] + [z for z, _ in near] + [None] + [r for _, r in near]
        keys = [z4_ref if r is None else r.at[0] for r in refs]
        values = [r4_ref if r is None else r.at[1] for r in refs]
        allowed = [row - col >= (p - ctx) * ROWS for p in places]
        zero = jnp.zeros((ROWS, HD), F32)
        for h in range(2):
            lanes = slice(h * HD, (h + 1) * HD)
            att_ref[:, lanes] = attend(
                q_ref[0, :, lanes], keys, values, allowed, lambda top: (top, 0.0, zero)
            )

    @pl.when(info[0] == 1)
    def _():
        places = [lax.rem(ctx + k, NCTX) for k in range(5)]
        places += [lax.rem(ctx + NCTX - k, NCTX) for k in range(1, 4)]
        refs = [span_ref] + [z for z, _ in near] + [None] + [r for _, r in near]
        keys = [r4_ref if r is None else r.at[0] for r in refs]
        values = [z4_ref if r is None else r.at[1] for r in refs]
        slot = slot_ref[...]
        request = jnp.where(owner_ref[...] == ctx, slot // PAGE, -1).astype(F32)
        page = lax.rem(slot, PAGE).astype(F32)
        in_page = (lax.rem(row, 2 * PAGE) == col // PAGE).astype(BF16)
        lens = lane_column(len_ref)
        pages = lax.broadcasted_iota(jnp.int32, (1, HD), 1) // (2 * PAGE)
        allowed = []
        for p in places:
            picked = jnp.concatenate([request, page] * 8, axis=0)
            picked = jnp.where(pages == p, picked, 0.0).astype(BF16)
            token = jnp.dot(picked, in_page, preferred_element_type=F32)
            position = token[1:2] * PAGE + lax.rem(col[:1], PAGE).astype(F32)
            allowed.append((token[:1] == row.astype(F32)) & (position < lens))
        key_new = new_ref[0].astype(F32)
        value_new = new_ref[1].astype(F32)
        for h in range(2):
            lanes = slice(h * HD, (h + 1) * HD)
            q = q_ref[0, :, lanes]
            fresh = jnp.sum(q.astype(F32) * key_new, axis=1, keepdims=True) * SCALE
            summed = jnp.concatenate([theirs_ref[0, h], mine_ref[0, h]], axis=0)
            stats = jnp.concatenate([theirs_ref[1, h], mine_ref[1, h]], axis=0)
            highest, total = stats[:, :1], stats[:, HALF : HALF + 1]

            def start(top):
                top = jnp.maximum(jnp.maximum(top, fresh), highest)
                old = jnp.exp(highest - top)
                new = jnp.exp(fresh - top)
                rounded = new.astype(BF16).astype(F32)
                return top, total * old + new, summed * old + rounded * value_new

            att_ref[:, lanes] = attend(q, keys, values, allowed, start)
    for n, ref in enumerate((s2l_ref, s2h_ref)):
        for m in range(2):
            ref[m] = product(info, att_ref, w_ref, 2, 2 * n + m).astype(BF16)


def product(info, att_ref, w_ref, k, j):
    start = pl.multiple_of(chunk(info, info[1] + k, j) * WIDE, WIDE)
    return jnp.dot(att_ref[...], w_ref[:, pl.ds(start, WIDE)], preferred_element_type=F32)


def output_kernel(info, att_ref, w_ref, s0_ref, s1l_ref, s1h_ref, s3l_ref, s3h_ref):
    for k, refs in ((1, (s1l_ref, s1h_ref)), (3, (s3l_ref, s3h_ref))):
        for j in range(SIDE):
            refs[j // 2][j % 2] = product(info, att_ref, w_ref, k, j).astype(BF16)
    for j in range(SIDE):
        s0_ref[j] = product(info, att_ref, w_ref, 0, j)


def add_kernel(own_ref, got_ref, out_ref):
    out_ref[...] = (own_ref[...].astype(F32) + got_ref[...].astype(F32)).astype(BF16)


def fold_kernel(s0_ref, ll_ref, lh_ref, rl_ref, rh_ref, low_ref, high_ref):
    for n, (left, right, out) in enumerate(((ll_ref, rl_ref, low_ref), (lh_ref, rh_ref, high_ref))):
        total = s0_ref[2 * n : 2 * n + 2] + left[...].astype(F32) + right[...].astype(F32)
        out[...] = total.astype(BF16)


def line_kernel(
    low_ref, high_ref, ll_ref, lh_ref, rl_ref, rh_ref, fl_ref, fh_ref, out_low_ref, out_high_ref
):
    for own, far, left, right, out in (
        (low_ref, fl_ref, ll_ref, rl_ref, out_low_ref),
        (high_ref, fh_ref, lh_ref, rh_ref, out_high_ref),
    ):
        first = own[...].astype(F32) + far[...].astype(F32)
        second = left[...].astype(F32) + right[...].astype(F32)
        out[...] = (first + second).astype(BF16)


def place(info, sources, out_ref, sems):
    copies = []
    for k, low, high in sources:
        for j in range(SIDE):
            start = pl.multiple_of(chunk(info, info[1] + SIDE - k, j) * WIDE, WIDE)
            ref = (low, high)[j // 2].at[j % 2]
            copies.append(
                pltpu.make_async_copy(
                    ref, out_ref.at[:, pl.ds(start, WIDE)], sems.at[len(copies)]
                )
            )
            copies[-1].start()
    for copy in copies:
        copy.wait()


def place_near(info, tl_ref, th_ref, ll_ref, lh_ref, rl_ref, rh_ref, out_ref, sems):
    place(info, ((0, tl_ref, th_ref), (1, ll_ref, lh_ref), (3, rl_ref, rh_ref)), out_ref, sems)


def place_far(info, held_ref, fl_ref, fh_ref, out_ref, sems):
    place(info, ((2, fl_ref, fh_ref),), out_ref, sems)


def with_scalars(kernel):
    def wrapped(*refs):
        kernel([ref[0] for ref in refs[:5]], *refs[5:])

    wrapped.__name__ = kernel.__name__
    return wrapped


def call(kernel, outs, in_specs, out_specs, flops, *args, scratch=(), limit=24 << 20, aliases=None):
    if in_specs[0] is SMEM:
        kernel, in_specs, args = with_scalars(kernel), [SMEM] * 4 + in_specs, (*args[0], *args[1:])
        aliases = {n + 4: m for n, m in (aliases or {}).items()}
    size = sum(x.size * x.dtype.itemsize for x in args)
    return pl.pallas_call(
        kernel,
        out_shape=outs,
        in_specs=in_specs,
        out_specs=out_specs,
        scratch_shapes=list(scratch),
        input_output_aliases=aliases or {},
        compiler_params=pltpu.CompilerParams(vmem_limit_bytes=limit),
        cost_estimate=pl.CostEstimate(flops=flops, bytes_accessed=size, transcendentals=0),
        name=kernel.__name__,
    )(*args)


def body(hidden, queries, kv_weight, out_weight, cache, page_owner, page_slot, cached_len):
    group = lax.axis_index("group")
    ctx = lax.axis_index("ctx")
    rank = lax.axis_index("tp")
    high, low = rank // SIDE, rank % SIDE
    a = jnp.where(group == 0, high, low)
    b = jnp.where(group == 0, low, high)
    info = [x.astype(jnp.int32).reshape(1) for x in (group, a, b, ctx, rank % 2)]
    st = jax.ShapeDtypeStruct
    dma = pltpu.SemaphoreType.DMA
    both = (0, 1)
    swap = lambda x: routed(x, both, lambda g, c, t: (1 - g, c, t))

    h = hidden[0]
    near = [h] + [shift(h, 0, k) for k in range(1, SIDE)]
    held = (
        call(join_kernel, st((2, ROWS, WIDE), BF16), [VMEM] * 2, VMEM, 1000, *near[:2]),
        jnp.stack(near[2:]),
    )
    ll, lh, rl, rh, fl, fh = relay(*held, along_a)
    owners, slots, lens = page_owner[None], page_slot[None], cached_len[None]

    acc = call(
        project_first, st((ROWS, HD), F32), [SMEM] + [VMEM] * 3, VMEM, 70_000_000,
        info, *held, kv_weight,
    )
    acc = call(
        project_near, st((ROWS, HD), F32), [SMEM] + [VMEM] * 6, VMEM, 140_000_000,
        info, acc, ll, lh, rl, rh, kv_weight,
    )
    kv = call(
        project_far, st((ROWS, HD), BF16), [SMEM] + [VMEM] * 4, VMEM, 70_000_000,
        info, acc, fl, fh, kv_weight,
    )

    kv, queries = lax.optimization_barrier((kv, queries))
    other_queries = swap(queries)
    pair = routed(kv, both, lambda g, c, t: (g, c, t ^ 1))
    swapped = swap(kv)
    cross = routed(kv, both, lambda g, c, t: (1 - g, c, t ^ 1))
    cached = call(
        cache_rows, st((HALF // BLOCK, BLOCK, HD, 2 * HD), BF16), [SMEM, VMEM, HBM], VMEM, 1000,
        info, queries, cache, scratch=[dma((HALF // BLOCK,))], limit=49 << 20,
    )
    pair, cached = lax.optimization_barrier((pair, cached))
    span, new, part = call(
        pack_kernel, [st((2, ROWS, HD), BF16)] * 2 + [st((ROWS, HD), BF16)],
        [SMEM] + [VMEM] * 4, [VMEM] * 3, 1000, info, kv, pair, swapped, cross,
    )

    def along_z(block, k):
        return routed(
            block, both, lambda g, c, t: (g, (c + (k if g == 0 else NCTX - k)) % NCTX, t)
        )

    zs = [along_z(x, k) for k, x in ((1, span), (2, span), (3, span), (4, part))]
    tied, zs[3] = lax.optimization_barrier((queries, zs[3]))
    old = call(
        cache_kernel, st((2, 2, HALF, HD), F32), [SMEM] + [VMEM] * 6, VMEM, 1000,
        info, tied, other_queries, cached, lens, owners, slots,
        scratch=[pltpu.VMEM((HALF, 2 * HD), BF16), pltpu.VMEM((ROWS, HD), F32)],
    )
    other_old = swap(old)

    rs = [swap(z) for z in zs]
    small = st((2, ROWS, WIDE), BF16)
    att, s2l, s2h = call(
        finish_kernel, [st((ROWS, 2 * HD), BF16), small, small],
        [SMEM] + [VMEM] * 17, [VMEM] * 3, 300_000_000,
        info, queries, span, new, *zs, *rs, lens, owners, slots, old, other_old, out_weight,
    )
    s0, s1l, s1h, s3l, s3h = call(
        output_kernel, [st((SIDE, ROWS, WIDE), F32)] + [small] * 4,
        [SMEM, VMEM, VMEM], [VMEM] * 5, 400_000_000, info, att, out_weight,
    )
    to_right = shift(s2l, 1, 0)
    to_left = shift(s2h, -1, 0)
    lh = shift(s1h, 1, 0)
    rl = shift(s3l, -1, 0)
    add = lambda x, y: call(add_kernel, small, [VMEM] * 2, VMEM, 1000, x, y)
    ll = shift(add(s1l, to_right), 1, 0)
    rh = shift(add(s3h, to_left), -1, 0)
    line = call(fold_kernel, [small] * 2, [VMEM] * 5, [VMEM] * 2, 1000, s0, ll, lh, rl, rh)
    line = call(
        line_kernel, [small] * 2, [VMEM] * 8, [VMEM] * 2, 1000, *line, *relay(*line, along_b)
    )
    ll, lh, rl, rh, fl, fh = relay(*line, along_a)
    whole = st((ROWS, RANKS * WIDE), BF16)
    out = call(
        place_near, whole, [SMEM] + [VMEM] * 6, HBM, 1000, info, *line, ll, lh, rl, rh,
        scratch=[dma((3 * SIDE,))],
    )
    out = call(
        place_far, whole, [SMEM, HBM, VMEM, VMEM], HBM, 1000, info, out, fl, fh,
        scratch=[dma((SIDE,))], aliases={1: 0},
    )
    return out[None]


def solution(mesh):
    return jax.shard_map(
        body,
        mesh=mesh,
        in_specs=(
            P("group", "ctx", "tp"),
            P("group", "ctx", "tp"),
            P(None, "tp"),
            P("tp", None),
            P("ctx", None, "tp"),
            P(),
            P(),
            P("ctx"),
        ),
        out_specs=P("group", "ctx", None),
        check_vma=False,
    )
```

```python
import jax
import jax.numpy as jnp
from jax import lax
from jax.experimental import pallas as pl
from jax.experimental.pallas import tpu as pltpu
from jax.sharding import PartitionSpec as P

HD = 128
PAGE = 8
SIDE = 4
RANKS = 16
NCTX = 8
ROWS = 128
WIDE = 512
BLOCK = 32
HALF = 64
SCALE = HD ** -0.5
NEG = -1e30
VMEM = pl.BlockSpec(memory_space=pltpu.VMEM)
SMEM = pl.BlockSpec(memory_space=pltpu.SMEM)
HBM = pl.BlockSpec(memory_space=pltpu.HBM)
F32 = jnp.float32
BF16 = jnp.bfloat16


def rank_of(group, a, b):
    return SIDE * a + b if group == 0 else SIDE * b + a


def tp_route(step_a, step_b):
    route = []
    for group in range(2):
        for a in range(SIDE):
            for b in range(SIDE):
                to = rank_of(group, (a + step_a) % SIDE, (b + step_b) % SIDE)
                route.append((group * RANKS + rank_of(group, a, b), group * RANKS + to))
    return route


def shift(block, step_a, step_b):
    return lax.ppermute(block, ("group", "tp"), tp_route(step_a, step_b))


def routed(block, groups, target):
    route = []
    for group in groups:
        for c in range(NCTX):
            for t in range(RANKS):
                g2, c2, t2 = target(group, c, t)
                route.append(((group * NCTX + c) * RANKS + t, (g2 * NCTX + c2) * RANKS + t2))
    return lax.ppermute(block, ("group", "ctx", "tp"), route)


def chunk(info, a, b):
    a, b = lax.rem(a, SIDE), lax.rem(b, SIDE)
    return jnp.where(info[0] == 0, SIDE * a + b, SIDE * b + a)


def behind(info, k, j):
    return chunk(info, info[1] + SIDE - k, info[2] + SIDE - j)


def nt(x, y):
    return lax.dot_general(x, y, (((1,), (1,)), ((), ())), preferred_element_type=F32)


def relay(low, high, step):
    left_low = step(low, 1)
    right_high = step(high, -1)
    left_high = step(high, 1)
    right_low = step(low, -1)
    far_low = step(left_low, 1)
    far_high = step(right_high, -1)
    return left_low, left_high, right_low, right_high, far_low, far_high


def along_a(block, k):
    return shift(block, k, 0)


def along_b(block, k):
    return shift(block, 0, k)


def lane_column(ref):
    return jnp.broadcast_to(ref[...].astype(F32), (HD, HD)).T


def cache_rows(info, order_ref, cache_ref, out_ref, sems):
    base = info[0] * HALF
    copies = []
    for i in range(HALF // BLOCK):
        start = pl.multiple_of(base + i * BLOCK, BLOCK)
        copies.append(
            pltpu.make_async_copy(cache_ref.at[pl.ds(start, BLOCK)], out_ref.at[i], sems.at[i])
        )
        copies[-1].start()
    for copy in copies:
        copy.wait()


def cache_kernel(
    info, q_ref, other_ref, buf, len_ref, owner_ref, slot_ref, out_ref, q_buf, open_buf
):
    base = info[0] * HALF
    steps = HALF // BLOCK

    @pl.when(info[0] == 0)
    def _():
        q_buf[...] = other_ref[0, :HALF, :]

    @pl.when(info[0] == 1)
    def _():
        q_buf[...] = q_ref[0, HALF:, :]

    request = lax.broadcasted_iota(jnp.int32, (ROWS, HD), 0)
    column = lax.broadcasted_iota(jnp.int32, (ROWS, HD), 1)
    slot = slot_ref[...]
    row_hit = (owner_ref[...] == info[3]) & (slot // PAGE == request)
    col_hit = request // PAGE == lax.rem(slot, PAGE)
    filled = nt(row_hit.astype(BF16), col_hit.astype(BF16))
    inside = column.astype(F32) < lane_column(len_ref)
    open_buf[...] = jnp.where(inside & (filled < 0.5), 1.0, 0.0)

    shape = (BLOCK, HD, 2 * BLOCK)
    own_key = lax.broadcasted_iota(jnp.int32, shape, 0) == lax.rem(
        lax.broadcasted_iota(jnp.int32, shape, 2), BLOCK
    )
    row_of = lax.rem(lax.broadcasted_iota(jnp.int32, (2 * BLOCK, HD), 0), BLOCK)
    lane = lax.broadcasted_iota(jnp.int32, (2 * BLOCK, HD), 1)

    def step(i, carry):
        rows = pl.ds(pl.multiple_of(i * BLOCK, BLOCK), BLOCK)
        q = q_buf[rows, :]
        q = jnp.concatenate([q[:, :HD], q[:, HD:]], axis=0)
        keys = buf[i, :, :, :HD].reshape(BLOCK * HD, HD)
        values = buf[i, :, :, HD:].reshape(BLOCK * HD, HD)
        wide = nt(keys, q).reshape(shape)
        scores = jnp.sum(jnp.where(own_key, wide, 0.0), axis=0).T * SCALE
        open_ = open_buf[pl.ds(pl.multiple_of(base + i * BLOCK, BLOCK), BLOCK), :]
        allowed = jnp.concatenate([open_, open_], axis=0) > 0.5
        scores = jnp.where(allowed, scores, NEG)
        top = jnp.max(scores, axis=1, keepdims=True)
        weights = jnp.where(allowed, jnp.exp(scores - top), 0.0)
        total = jnp.sum(weights, axis=1, keepdims=True)
        spread = jnp.concatenate(
            [jnp.where(row_of == r, weights, 0.0).astype(BF16) for r in range(BLOCK)], axis=1
        )
        summed = jnp.dot(spread, values, preferred_element_type=F32)
        stats = jnp.where(lane < HALF, top, total)
        for h in range(2):
            part = slice(h * BLOCK, (h + 1) * BLOCK)
            out_ref[0, h, rows, :] = summed[part]
            out_ref[1, h, rows, :] = stats[part]
        return carry

    lax.fori_loop(0, steps, step, 0)


def join_kernel(first_ref, second_ref, out_ref):
    out_ref[0] = first_ref[...]
    out_ref[1] = second_ref[...]


def project_first(info, low_ref, high_ref, w_ref, acc_ref):
    total = jnp.zeros((ROWS, HD), F32)
    for j in range(SIDE):
        ref = (low_ref, high_ref)[j // 2]
        start = pl.multiple_of(behind(info, 0, j) * WIDE, WIDE)
        total += jnp.dot(ref[j % 2], w_ref[pl.ds(start, WIDE), :], preferred_element_type=F32)
    acc_ref[...] = total


def project_near(info, acc_ref, l0_ref, l1_ref, r0_ref, r1_ref, w_ref, out_ref):
    total = acc_ref[...]
    for k, refs in ((1, (l0_ref, l1_ref)), (3, (r0_ref, r1_ref))):
        for j in range(SIDE):
            start = pl.multiple_of(behind(info, k, j) * WIDE, WIDE)
            total += jnp.dot(
                refs[j // 2][j % 2], w_ref[pl.ds(start, WIDE), :], preferred_element_type=F32
            )
    out_ref[...] = total


def project_far(info, acc_ref, f0_ref, f1_ref, w_ref, kv_ref):
    total = acc_ref[...]
    for j in range(SIDE):
        ref = (f0_ref, f1_ref)[j // 2]
        start = pl.multiple_of(behind(info, 2, j) * WIDE, WIDE)
        total += jnp.dot(ref[j % 2], w_ref[pl.ds(start, WIDE), :], preferred_element_type=F32)
    kv_ref[...] = total.astype(BF16)


def pack_kernel(info, own_ref, pair_ref, swap_ref, cross_ref, span_ref, new_ref, half_ref):
    def put(ref, first, second):
        ref[0] = first[...]
        ref[1] = second[...]

    @pl.when(info[4] == 0)
    def _():
        put(new_ref, own_ref, pair_ref)

    @pl.when(info[4] == 1)
    def _():
        put(new_ref, pair_ref, own_ref)

    @pl.when(info[0] == 0)
    def _():
        span_ref[...] = new_ref[...]
        half_ref[...] = new_ref[0]

    @pl.when((info[0] == 1) & (info[4] == 0))
    def _():
        put(span_ref, swap_ref, cross_ref)
        half_ref[...] = cross_ref[...]

    @pl.when((info[0] == 1) & (info[4] == 1))
    def _():
        put(span_ref, cross_ref, swap_ref)
        half_ref[...] = swap_ref[...]


def attend(q, keys, values, allowed, start):
    scores = [jnp.where(m, nt(q, k[...]) * SCALE, NEG) for m, k in zip(allowed, keys)]
    top = scores[0]
    for s in scores[1:]:
        top = jnp.maximum(top, s)
    top = jnp.max(top, axis=1, keepdims=True)
    top, total, summed = start(top)
    sums = jnp.zeros((2 * ROWS, HD), F32)
    for s, m, v in zip(scores, allowed, values):
        w = jnp.where(m, jnp.exp(s - top), 0.0)
        sums += w
        summed += jnp.dot(w.astype(BF16), v[...], preferred_element_type=F32)
    total += jnp.sum(sums, axis=1, keepdims=True)
    return (summed / total).astype(BF16)


def finish_kernel(
    info, q_ref, span_ref, new_ref, z1_ref, z2_ref, z3_ref, z4_ref, r1_ref, r2_ref, r3_ref, r4_ref,
    len_ref, owner_ref, slot_ref, mine_ref, theirs_ref, w_ref,
    att_ref, s2l_ref, s2h_ref,
):
    row = lax.rem(lax.broadcasted_iota(jnp.int32, (2 * ROWS, HD), 0), ROWS)
    col = lax.broadcasted_iota(jnp.int32, (2 * ROWS, HD), 1)
    q = jnp.concatenate([q_ref[0, :, :HD], q_ref[0, :, HD:]], axis=0)

    def put(out):
        att_ref[:, :HD] = out[:ROWS]
        att_ref[:, HD:] = out[ROWS:]

    ctx = info[3]
    near = [(z1_ref, r1_ref), (z2_ref, r2_ref), (z3_ref, r3_ref)]

    @pl.when(info[0] == 0)
    def _():
        places = [lax.rem(ctx + NCTX - k, NCTX) for k in range(5)]
        places += [lax.rem(ctx + k, NCTX) for k in range(1, 4)]
        refs = [span_ref] + [z for z, _ in near] + [None] + [r for _, r in near]
        keys = [z4_ref if r is None else r.at[0] for r in refs]
        values = [r4_ref if r is None else r.at[1] for r in refs]
        allowed = [row - col >= (p - ctx) * ROWS for p in places]
        zero = jnp.zeros((2 * ROWS, HD), F32)
        put(attend(q, keys, values, allowed, lambda top: (top, 0.0, zero)))

    @pl.when(info[0] == 1)
    def _():
        places = [lax.rem(ctx + k, NCTX) for k in range(5)]
        places += [lax.rem(ctx + NCTX - k, NCTX) for k in range(1, 4)]
        refs = [span_ref] + [z for z, _ in near] + [None] + [r for _, r in near]
        keys = [r4_ref if r is None else r.at[0] for r in refs]
        values = [z4_ref if r is None else r.at[1] for r in refs]
        slot = slot_ref[...]
        request = jnp.where(owner_ref[...] == ctx, slot // PAGE, -1).astype(F32)
        page = lax.rem(slot, PAGE).astype(F32)
        in_page = (lax.rem(row[:ROWS], 2 * PAGE) == col[:ROWS] // PAGE).astype(BF16)
        lens = jnp.concatenate([lane_column(len_ref)] * 2, axis=0)
        pages = lax.broadcasted_iota(jnp.int32, (1, HD), 1) // (2 * PAGE)
        allowed = []
        for p in places:
            picked = jnp.concatenate([request, page] * 8, axis=0)
            picked = jnp.where(pages == p, picked, 0.0).astype(BF16)
            token = jnp.dot(picked, in_page, preferred_element_type=F32)
            position = token[1:2] * PAGE + lax.rem(col[:1], PAGE).astype(F32)
            allowed.append((token[:1] == row.astype(F32)) & (position < lens))
        key_new = jnp.concatenate([new_ref[0].astype(F32)] * 2, axis=0)
        value_new = jnp.concatenate([new_ref[1].astype(F32)] * 2, axis=0)
        fresh = jnp.sum(q.astype(F32) * key_new, axis=1, keepdims=True) * SCALE
        pieces = [(ref, h) for h in range(2) for ref in (theirs_ref, mine_ref)]
        summed = jnp.concatenate([ref[0, h] for ref, h in pieces], axis=0)
        stats = jnp.concatenate([ref[1, h] for ref, h in pieces], axis=0)
        highest, total = stats[:, :1], stats[:, HALF : HALF + 1]

        def start(top):
            top = jnp.maximum(jnp.maximum(top, fresh), highest)
            old = jnp.exp(highest - top)
            new = jnp.exp(fresh - top)
            rounded = new.astype(BF16).astype(F32)
            return top, total * old + new, summed * old + rounded * value_new

        put(attend(q, keys, values, allowed, start))

    for n, ref in enumerate((s2l_ref, s2h_ref)):
        for m in range(2):
            ref[m] = product(info, att_ref, w_ref, 2, 2 * n + m).astype(BF16)


def product(info, att_ref, w_ref, k, j):
    start = pl.multiple_of(chunk(info, info[1] + k, j) * WIDE, WIDE)
    return jnp.dot(att_ref[...], w_ref[:, pl.ds(start, WIDE)], preferred_element_type=F32)


def output_kernel(info, att_ref, w_ref, s0_ref, s1l_ref, s1h_ref, s3l_ref, s3h_ref):
    for k, refs in ((1, (s1l_ref, s1h_ref)), (3, (s3l_ref, s3h_ref))):
        for j in range(SIDE):
            refs[j // 2][j % 2] = product(info, att_ref, w_ref, k, j).astype(BF16)
    for j in range(SIDE):
        s0_ref[j] = product(info, att_ref, w_ref, 0, j)


def add_kernel(own_ref, got_ref, out_ref):
    out_ref[...] = (own_ref[...].astype(F32) + got_ref[...].astype(F32)).astype(BF16)


def fold_kernel(s0_ref, ll_ref, lh_ref, rl_ref, rh_ref, low_ref, high_ref):
    for n, (left, right, out) in enumerate(((ll_ref, rl_ref, low_ref), (lh_ref, rh_ref, high_ref))):
        total = s0_ref[2 * n : 2 * n + 2] + left[...].astype(F32) + right[...].astype(F32)
        out[...] = total.astype(BF16)


def line_kernel(
    low_ref, high_ref, ll_ref, lh_ref, rl_ref, rh_ref, fl_ref, fh_ref, out_low_ref, out_high_ref
):
    for own, far, left, right, out in (
        (low_ref, fl_ref, ll_ref, rl_ref, out_low_ref),
        (high_ref, fh_ref, lh_ref, rh_ref, out_high_ref),
    ):
        first = own[...].astype(F32) + far[...].astype(F32)
        second = left[...].astype(F32) + right[...].astype(F32)
        out[...] = (first + second).astype(BF16)


def place(info, sources, out_ref, sems):
    copies = []
    for k, low, high in sources:
        for j in range(SIDE):
            start = pl.multiple_of(chunk(info, info[1] + SIDE - k, j) * WIDE, WIDE)
            ref = (low, high)[j // 2].at[j % 2]
            copies.append(
                pltpu.make_async_copy(
                    ref, out_ref.at[:, pl.ds(start, WIDE)], sems.at[len(copies)]
                )
            )
            copies[-1].start()
    for copy in copies:
        copy.wait()


def place_near(info, tl_ref, th_ref, ll_ref, lh_ref, rl_ref, rh_ref, out_ref, sems):
    place(info, ((0, tl_ref, th_ref), (1, ll_ref, lh_ref), (3, rl_ref, rh_ref)), out_ref, sems)


def place_far(info, held_ref, fl_ref, fh_ref, out_ref, sems):
    place(info, ((2, fl_ref, fh_ref),), out_ref, sems)


def with_scalars(kernel):
    def wrapped(*refs):
        kernel([ref[0] for ref in refs[:5]], *refs[5:])

    wrapped.__name__ = kernel.__name__
    return wrapped


def call(kernel, outs, in_specs, out_specs, flops, *args, scratch=(), limit=24 << 20, aliases=None):
    if in_specs[0] is SMEM:
        kernel, in_specs, args = with_scalars(kernel), [SMEM] * 4 + in_specs, (*args[0], *args[1:])
        aliases = {n + 4: m for n, m in (aliases or {}).items()}
    size = sum(x.size * x.dtype.itemsize for x in args)
    return pl.pallas_call(
        kernel,
        out_shape=outs,
        in_specs=in_specs,
        out_specs=out_specs,
        scratch_shapes=list(scratch),
        input_output_aliases=aliases or {},
        compiler_params=pltpu.CompilerParams(vmem_limit_bytes=limit),
        cost_estimate=pl.CostEstimate(flops=flops, bytes_accessed=size, transcendentals=0),
        name=kernel.__name__,
    )(*args)


def body(hidden, queries, kv_weight, out_weight, cache, page_owner, page_slot, cached_len):
    group = lax.axis_index("group")
    ctx = lax.axis_index("ctx")
    rank = lax.axis_index("tp")
    high, low = rank // SIDE, rank % SIDE
    a = jnp.where(group == 0, high, low)
    b = jnp.where(group == 0, low, high)
    info = [x.astype(jnp.int32).reshape(1) for x in (group, a, b, ctx, rank % 2)]
    st = jax.ShapeDtypeStruct
    dma = pltpu.SemaphoreType.DMA
    both = (0, 1)
    swap = lambda x: routed(x, both, lambda g, c, t: (1 - g, c, t))

    h = hidden[0]
    near = [h] + [shift(h, 0, k) for k in range(1, SIDE)]
    held = (
        call(join_kernel, st((2, ROWS, WIDE), BF16), [VMEM] * 2, VMEM, 1000, *near[:2]),
        jnp.stack(near[2:]),
    )
    ll, lh, rl, rh, fl, fh = relay(*held, along_a)
    owners, slots, lens = page_owner[None], page_slot[None], cached_len[None]

    acc = call(
        project_first, st((ROWS, HD), F32), [SMEM] + [VMEM] * 3, VMEM, 70_000_000,
        info, *held, kv_weight,
    )
    acc = call(
        project_near, st((ROWS, HD), F32), [SMEM] + [VMEM] * 6, VMEM, 140_000_000,
        info, acc, ll, lh, rl, rh, kv_weight,
    )
    kv = call(
        project_far, st((ROWS, HD), BF16), [SMEM] + [VMEM] * 4, VMEM, 70_000_000,
        info, acc, fl, fh, kv_weight,
    )

    kv, queries = lax.optimization_barrier((kv, queries))
    other_queries = swap(queries)
    pair = routed(kv, both, lambda g, c, t: (g, c, t ^ 1))
    swapped = swap(kv)
    cross = routed(kv, both, lambda g, c, t: (1 - g, c, t ^ 1))
    cached = call(
        cache_rows, st((HALF // BLOCK, BLOCK, HD, 2 * HD), BF16), [SMEM, VMEM, HBM], VMEM, 1000,
        info, queries, cache, scratch=[dma((HALF // BLOCK,))], limit=49 << 20,
    )
    pair, cached = lax.optimization_barrier((pair, cached))
    span, new, part = call(
        pack_kernel, [st((2, ROWS, HD), BF16)] * 2 + [st((ROWS, HD), BF16)],
        [SMEM] + [VMEM] * 4, [VMEM] * 3, 1000, info, kv, pair, swapped, cross,
    )

    def along_z(block, k):
        return routed(
            block, both, lambda g, c, t: (g, (c + (k if g == 0 else NCTX - k)) % NCTX, t)
        )

    zs = [along_z(x, k) for k, x in ((1, span), (2, span), (3, span), (4, part))]
    tied, zs[3] = lax.optimization_barrier((queries, zs[3]))
    old = call(
        cache_kernel, st((2, 2, HALF, HD), F32), [SMEM] + [VMEM] * 6, VMEM, 1000,
        info, tied, other_queries, cached, lens, owners, slots,
        scratch=[pltpu.VMEM((HALF, 2 * HD), BF16), pltpu.VMEM((ROWS, HD), F32)],
    )
    other_old = swap(old)

    rs = [swap(z) for z in zs]
    small = st((2, ROWS, WIDE), BF16)
    att, s2l, s2h = call(
        finish_kernel, [st((ROWS, 2 * HD), BF16), small, small],
        [SMEM] + [VMEM] * 17, [VMEM] * 3, 300_000_000,
        info, queries, span, new, *zs, *rs, lens, owners, slots, old, other_old, out_weight,
    )
    s0, s1l, s1h, s3l, s3h = call(
        output_kernel, [st((SIDE, ROWS, WIDE), F32)] + [small] * 4,
        [SMEM, VMEM, VMEM], [VMEM] * 5, 400_000_000, info, att, out_weight,
    )
    to_right = shift(s2l, 1, 0)
    to_left = shift(s2h, -1, 0)
    lh = shift(s1h, 1, 0)
    rl = shift(s3l, -1, 0)
    add = lambda x, y: call(add_kernel, small, [VMEM] * 2, VMEM, 1000, x, y)
    ll = shift(add(s1l, to_right), 1, 0)
    rh = shift(add(s3h, to_left), -1, 0)
    line = call(fold_kernel, [small] * 2, [VMEM] * 5, [VMEM] * 2, 1000, s0, ll, lh, rl, rh)
    line = call(
        line_kernel, [small] * 2, [VMEM] * 8, [VMEM] * 2, 1000, *line, *relay(*line, along_b)
    )
    ll, lh, rl, rh, fl, fh = relay(*line, along_a)
    whole = st((ROWS, RANKS * WIDE), BF16)
    out = call(
        place_near, whole, [SMEM] + [VMEM] * 6, HBM, 1000, info, *line, ll, lh, rl, rh,
        scratch=[dma((3 * SIDE,))],
    )
    out = call(
        place_far, whole, [SMEM, HBM, VMEM, VMEM], HBM, 1000, info, out, fl, fh,
        scratch=[dma((SIDE,))], aliases={1: 0},
    )
    return out[None]


def solution(mesh):
    return jax.shard_map(
        body,
        mesh=mesh,
        in_specs=(
            P("group", "ctx", "tp"),
            P("group", "ctx", "tp"),
            P(None, "tp"),
            P("tp", None),
            P("ctx", None, "tp"),
            P(),
            P(),
            P("ctx"),
        ),
        out_specs=P("group", "ctx", None),
        check_vma=False,
    )
```

```python
import jax
import jax.numpy as jnp
from jax import lax
from jax.experimental import pallas as pl
from jax.experimental.pallas import tpu as pltpu
from jax.sharding import PartitionSpec as P

HD = 128
PAGE = 8
SIDE = 4
RANKS = 16
NCTX = 8
ROWS = 128
WIDE = 512
BLOCK = 32
HALF = 64
SCALE = HD ** -0.5
NEG = -1e30
VMEM = pl.BlockSpec(memory_space=pltpu.VMEM)
SMEM = pl.BlockSpec(memory_space=pltpu.SMEM)
HBM = pl.BlockSpec(memory_space=pltpu.HBM)
F32 = jnp.float32
BF16 = jnp.bfloat16


def rank_of(group, a, b):
    return SIDE * a + b if group == 0 else SIDE * b + a


def tp_route(step_a, step_b):
    route = []
    for group in range(2):
        for a in range(SIDE):
            for b in range(SIDE):
                to = rank_of(group, (a + step_a) % SIDE, (b + step_b) % SIDE)
                route.append((group * RANKS + rank_of(group, a, b), group * RANKS + to))
    return route


def shift(block, step_a, step_b):
    return lax.ppermute(block, ("group", "tp"), tp_route(step_a, step_b))


def routed(block, groups, target):
    route = []
    for group in groups:
        for c in range(NCTX):
            for t in range(RANKS):
                g2, c2, t2 = target(group, c, t)
                route.append(((group * NCTX + c) * RANKS + t, (g2 * NCTX + c2) * RANKS + t2))
    return lax.ppermute(block, ("group", "ctx", "tp"), route)


def chunk(info, a, b):
    a, b = lax.rem(a, SIDE), lax.rem(b, SIDE)
    return jnp.where(info[0] == 0, SIDE * a + b, SIDE * b + a)


def behind(info, k, j):
    return chunk(info, info[1] + SIDE - k, info[2] + SIDE - j)


def nt(x, y):
    return lax.dot_general(x, y, (((1,), (1,)), ((), ())), preferred_element_type=F32)


def relay(low, high, step):
    left_low = step(low, 1)
    right_high = step(high, -1)
    left_high = step(high, 1)
    right_low = step(low, -1)
    far_low = step(left_low, 1)
    far_high = step(right_high, -1)
    return left_low, left_high, right_low, right_high, far_low, far_high


def along_a(block, k):
    return shift(block, k, 0)


def along_b(block, k):
    return shift(block, 0, k)


def lane_column(ref):
    return jnp.broadcast_to(ref[...].astype(F32), (HD, HD)).T


def cache_rows(info, order_ref, cache_ref, out_ref, sems):
    base = info[0] * HALF
    copies = []
    for i in range(HALF // BLOCK):
        start = pl.multiple_of(base + i * BLOCK, BLOCK)
        copies.append(
            pltpu.make_async_copy(cache_ref.at[pl.ds(start, BLOCK)], out_ref.at[i], sems.at[i])
        )
        copies[-1].start()
    for copy in copies:
        copy.wait()


def cache_kernel(
    info, q_ref, other_ref, buf, len_ref, owner_ref, slot_ref, out_ref, q_buf, open_buf
):
    base = info[0] * HALF
    steps = HALF // BLOCK

    @pl.when(info[0] == 0)
    def _():
        q_buf[...] = other_ref[0, :HALF, :]

    @pl.when(info[0] == 1)
    def _():
        q_buf[...] = q_ref[0, HALF:, :]

    request = lax.broadcasted_iota(jnp.int32, (ROWS, HD), 0)
    column = lax.broadcasted_iota(jnp.int32, (ROWS, HD), 1)
    slot = slot_ref[...]
    row_hit = (owner_ref[...] == info[3]) & (slot // PAGE == request)
    col_hit = request // PAGE == lax.rem(slot, PAGE)
    filled = nt(row_hit.astype(BF16), col_hit.astype(BF16))
    inside = column.astype(F32) < lane_column(len_ref)
    open_buf[...] = jnp.where(inside & (filled < 0.5), 1.0, 0.0)

    shape = (BLOCK, HD, 2 * BLOCK)
    own_key = lax.broadcasted_iota(jnp.int32, shape, 0) == lax.rem(
        lax.broadcasted_iota(jnp.int32, shape, 2), BLOCK
    )
    row_of = lax.rem(lax.broadcasted_iota(jnp.int32, (2 * BLOCK, HD), 0), BLOCK)
    lane = lax.broadcasted_iota(jnp.int32, (2 * BLOCK, HD), 1)

    def step(i, carry):
        rows = pl.ds(pl.multiple_of(i * BLOCK, BLOCK), BLOCK)
        q = q_buf[rows, :]
        q = jnp.concatenate([q[:, :HD], q[:, HD:]], axis=0)
        keys = buf[i, :, :, :HD].reshape(BLOCK * HD, HD)
        values = buf[i, :, :, HD:].reshape(BLOCK * HD, HD)
        wide = nt(keys, q).reshape(shape)
        scores = jnp.sum(jnp.where(own_key, wide, 0.0), axis=0).T * SCALE
        open_ = open_buf[pl.ds(pl.multiple_of(base + i * BLOCK, BLOCK), BLOCK), :]
        allowed = jnp.concatenate([open_, open_], axis=0) > 0.5
        scores = jnp.where(allowed, scores, NEG)
        top = jnp.max(scores, axis=1, keepdims=True)
        weights = jnp.where(allowed, jnp.exp(scores - top), 0.0)
        total = jnp.sum(weights, axis=1, keepdims=True)
        spread = jnp.concatenate(
            [jnp.where(row_of == r, weights, 0.0).astype(BF16) for r in range(BLOCK)], axis=1
        )
        summed = jnp.dot(spread, values, preferred_element_type=F32)
        stats = jnp.where(lane < HALF, top, total)
        for h in range(2):
            part = slice(h * BLOCK, (h + 1) * BLOCK)
            out_ref[0, h, rows, :] = summed[part]
            out_ref[1, h, rows, :] = stats[part]
        return carry

    lax.fori_loop(0, steps, step, 0)


def join_kernel(first_ref, second_ref, out_ref):
    out_ref[0] = first_ref[...]
    out_ref[1] = second_ref[...]


def project_first(info, low_ref, high_ref, w_ref, acc_ref):
    total = jnp.zeros((ROWS, HD), F32)
    for j in range(SIDE):
        ref = (low_ref, high_ref)[j // 2]
        start = pl.multiple_of(behind(info, 0, j) * WIDE, WIDE)
        total += jnp.dot(ref[j % 2], w_ref[pl.ds(start, WIDE), :], preferred_element_type=F32)
    acc_ref[...] = total


def project_near(info, acc_ref, l0_ref, l1_ref, r0_ref, r1_ref, w_ref, out_ref):
    total = acc_ref[...]
    for k, refs in ((1, (l0_ref, l1_ref)), (3, (r0_ref, r1_ref))):
        for j in range(SIDE):
            start = pl.multiple_of(behind(info, k, j) * WIDE, WIDE)
            total += jnp.dot(
                refs[j // 2][j % 2], w_ref[pl.ds(start, WIDE), :], preferred_element_type=F32
            )
    out_ref[...] = total


def project_far(info, acc_ref, f0_ref, f1_ref, w_ref, kv_ref):
    total = acc_ref[...]
    for j in range(SIDE):
        ref = (f0_ref, f1_ref)[j // 2]
        start = pl.multiple_of(behind(info, 2, j) * WIDE, WIDE)
        total += jnp.dot(ref[j % 2], w_ref[pl.ds(start, WIDE), :], preferred_element_type=F32)
    kv_ref[...] = total.astype(BF16)


def pack_kernel(info, own_ref, pair_ref, swap_ref, cross_ref, span_ref, new_ref, half_ref):
    def put(ref, first, second):
        ref[0] = first[...]
        ref[1] = second[...]

    @pl.when(info[4] == 0)
    def _():
        put(new_ref, own_ref, pair_ref)

    @pl.when(info[4] == 1)
    def _():
        put(new_ref, pair_ref, own_ref)

    @pl.when(info[0] == 0)
    def _():
        span_ref[...] = new_ref[...]
        half_ref[...] = new_ref[0]

    @pl.when((info[0] == 1) & (info[4] == 0))
    def _():
        put(span_ref, swap_ref, cross_ref)
        half_ref[...] = cross_ref[...]

    @pl.when((info[0] == 1) & (info[4] == 1))
    def _():
        put(span_ref, cross_ref, swap_ref)
        half_ref[...] = swap_ref[...]


def attend(q, keys, values, allowed, start):
    scores = [jnp.where(m, nt(q, k[...]) * SCALE, NEG) for m, k in zip(allowed, keys)]
    top = scores[0]
    for s in scores[1:]:
        top = jnp.maximum(top, s)
    top = jnp.max(top, axis=1, keepdims=True)
    top, total, summed = start(top)
    sums = jnp.zeros((2 * ROWS, HD), F32)
    for s, m, v in zip(scores, allowed, values):
        w = jnp.where(m, jnp.exp(s - top), 0.0)
        sums += w
        summed += jnp.dot(w.astype(BF16), v[...], preferred_element_type=F32)
    total += jnp.sum(sums, axis=1, keepdims=True)
    return (summed / total).astype(BF16)


def finish_kernel(
    info, q_ref, span_ref, new_ref, z1_ref, z2_ref, z3_ref, z4_ref, r1_ref, r2_ref, r3_ref, r4_ref,
    len_ref, owner_ref, slot_ref, mine_ref, theirs_ref, w_ref,
    att_ref, s2l_ref, s2h_ref,
):
    row = lax.rem(lax.broadcasted_iota(jnp.int32, (2 * ROWS, HD), 0), ROWS)
    col = lax.broadcasted_iota(jnp.int32, (2 * ROWS, HD), 1)
    q = jnp.concatenate([q_ref[0, :, :HD], q_ref[0, :, HD:]], axis=0)

    def put(out):
        att_ref[:, :HD] = out[:ROWS]
        att_ref[:, HD:] = out[ROWS:]

    ctx = info[3]
    near = [(z1_ref, r1_ref), (z2_ref, r2_ref), (z3_ref, r3_ref)]

    @pl.when(info[0] == 0)
    def _():
        places = [lax.rem(ctx + NCTX - k, NCTX) for k in range(5)]
        places += [lax.rem(ctx + k, NCTX) for k in range(1, 4)]
        refs = [span_ref] + [z for z, _ in near] + [None] + [r for _, r in near]
        keys = [z4_ref if r is None else r.at[0] for r in refs]
        values = [r4_ref if r is None else r.at[1] for r in refs]
        allowed = [row - col >= (p - ctx) * ROWS for p in places]
        zero = jnp.zeros((2 * ROWS, HD), F32)
        put(attend(q, keys, values, allowed, lambda top: (top, 0.0, zero)))

    @pl.when(info[0] == 1)
    def _():
        places = [lax.rem(ctx + k, NCTX) for k in range(5)]
        places += [lax.rem(ctx + NCTX - k, NCTX) for k in range(1, 4)]
        refs = [span_ref] + [z for z, _ in near] + [None] + [r for _, r in near]
        keys = [r4_ref if r is None else r.at[0] for r in refs]
        values = [z4_ref if r is None else r.at[1] for r in refs]
        slot = slot_ref[...]
        request = jnp.where(owner_ref[...] == ctx, slot // PAGE, -1).astype(F32)
        page = lax.rem(slot, PAGE).astype(F32)
        in_page = (lax.rem(row[:ROWS], 2 * PAGE) == col[:ROWS] // PAGE).astype(BF16)
        lens = jnp.concatenate([lane_column(len_ref)] * 2, axis=0)
        pages = lax.broadcasted_iota(jnp.int32, (1, HD), 1) // (2 * PAGE)
        allowed = []
        for p in places:
            picked = jnp.concatenate([request, page] * 8, axis=0)
            picked = jnp.where(pages == p, picked, 0.0).astype(BF16)
            token = jnp.dot(picked, in_page, preferred_element_type=F32)
            position = token[1:2] * PAGE + lax.rem(col[:1], PAGE).astype(F32)
            allowed.append((token[:1] == row.astype(F32)) & (position < lens))
        key_new = jnp.concatenate([new_ref[0].astype(F32)] * 2, axis=0)
        value_new = jnp.concatenate([new_ref[1].astype(F32)] * 2, axis=0)
        fresh = jnp.sum(q.astype(F32) * key_new, axis=1, keepdims=True) * SCALE
        pieces = [(ref, h) for h in range(2) for ref in (theirs_ref, mine_ref)]
        summed = jnp.concatenate([ref[0, h] for ref, h in pieces], axis=0)
        stats = jnp.concatenate([ref[1, h] for ref, h in pieces], axis=0)
        highest, total = stats[:, :1], stats[:, HALF : HALF + 1]

        def start(top):
            top = jnp.maximum(jnp.maximum(top, fresh), highest)
            old = jnp.exp(highest - top)
            new = jnp.exp(fresh - top)
            rounded = new.astype(BF16).astype(F32)
            return top, total * old + new, summed * old + rounded * value_new

        put(attend(q, keys, values, allowed, start))

    for n, ref in enumerate((s2l_ref, s2h_ref)):
        for m in range(2):
            ref[m] = product(info, att_ref, w_ref, 2, 2 * n + m).astype(BF16)


def product(info, att_ref, w_ref, k, j):
    start = pl.multiple_of(chunk(info, info[1] + k, j) * WIDE, WIDE)
    return jnp.dot(att_ref[...], w_ref[:, pl.ds(start, WIDE)], preferred_element_type=F32)


def output_kernel(info, att_ref, w_ref, s0_ref, s1l_ref, s1h_ref, s3l_ref, s3h_ref):
    for k, refs in ((1, (s1l_ref, s1h_ref)), (3, (s3l_ref, s3h_ref))):
        for j in range(SIDE):
            refs[j // 2][j % 2] = product(info, att_ref, w_ref, k, j).astype(BF16)
    for j in range(SIDE):
        s0_ref[j] = product(info, att_ref, w_ref, 0, j)


def add_kernel(own_ref, got_ref, out_ref):
    out_ref[...] = (own_ref[...].astype(F32) + got_ref[...].astype(F32)).astype(BF16)


def fold_kernel(s0_ref, ll_ref, lh_ref, rl_ref, rh_ref, low_ref, high_ref):
    for n, (left, right, out) in enumerate(((ll_ref, rl_ref, low_ref), (lh_ref, rh_ref, high_ref))):
        total = s0_ref[2 * n : 2 * n + 2] + left[...].astype(F32) + right[...].astype(F32)
        out[...] = total.astype(BF16)


def line_kernel(
    low_ref, high_ref, ll_ref, lh_ref, rl_ref, rh_ref, fl_ref, fh_ref, out_low_ref, out_high_ref
):
    for own, far, left, right, out in (
        (low_ref, fl_ref, ll_ref, rl_ref, out_low_ref),
        (high_ref, fh_ref, lh_ref, rh_ref, out_high_ref),
    ):
        first = own[...].astype(F32) + far[...].astype(F32)
        second = left[...].astype(F32) + right[...].astype(F32)
        out[...] = (first + second).astype(BF16)


def place(info, sources, out_ref, sems):
    copies = []
    for k, low, high in sources:
        for j in range(SIDE):
            start = pl.multiple_of(chunk(info, info[1] + SIDE - k, j) * WIDE, WIDE)
            ref = (low, high)[j // 2].at[j % 2]
            copies.append(
                pltpu.make_async_copy(
                    ref, out_ref.at[:, pl.ds(start, WIDE)], sems.at[len(copies)]
                )
            )
            copies[-1].start()
    for copy in copies:
        copy.wait()


def place_near(info, tl_ref, th_ref, ll_ref, lh_ref, rl_ref, rh_ref, out_ref, sems):
    place(info, ((0, tl_ref, th_ref), (1, ll_ref, lh_ref), (3, rl_ref, rh_ref)), out_ref, sems)


def place_far(half, info, held_ref, far_ref, out_ref, sems):
    copies = []
    for m in range(2):
        start = pl.multiple_of(chunk(info, info[1] + 2, 2 * half + m) * WIDE, WIDE)
        copies.append(
            pltpu.make_async_copy(far_ref.at[m], out_ref.at[:, pl.ds(start, WIDE)], sems.at[m])
        )
        copies[-1].start()
    for copy in copies:
        copy.wait()


def place_low(*refs):
    place_far(0, *refs)


def place_high(*refs):
    place_far(1, *refs)


def with_scalars(kernel):
    def wrapped(*refs):
        kernel([ref[0] for ref in refs[:5]], *refs[5:])

    wrapped.__name__ = kernel.__name__
    return wrapped


def call(kernel, outs, in_specs, out_specs, flops, *args, scratch=(), limit=24 << 20, aliases=None):
    if in_specs[0] is SMEM:
        kernel, in_specs, args = with_scalars(kernel), [SMEM] * 4 + in_specs, (*args[0], *args[1:])
        aliases = {n + 4: m for n, m in (aliases or {}).items()}
    size = sum(x.size * x.dtype.itemsize for x in args)
    return pl.pallas_call(
        kernel,
        out_shape=outs,
        in_specs=in_specs,
        out_specs=out_specs,
        scratch_shapes=list(scratch),
        input_output_aliases=aliases or {},
        compiler_params=pltpu.CompilerParams(vmem_limit_bytes=limit),
        cost_estimate=pl.CostEstimate(flops=flops, bytes_accessed=size, transcendentals=0),
        name=kernel.__name__,
    )(*args)


def body(hidden, queries, kv_weight, out_weight, cache, page_owner, page_slot, cached_len):
    group = lax.axis_index("group")
    ctx = lax.axis_index("ctx")
    rank = lax.axis_index("tp")
    high, low = rank // SIDE, rank % SIDE
    a = jnp.where(group == 0, high, low)
    b = jnp.where(group == 0, low, high)
    info = [x.astype(jnp.int32).reshape(1) for x in (group, a, b, ctx, rank % 2)]
    st = jax.ShapeDtypeStruct
    dma = pltpu.SemaphoreType.DMA
    both = (0, 1)
    swap = lambda x: routed(x, both, lambda g, c, t: (1 - g, c, t))

    h = hidden[0]
    near = [h] + [shift(h, 0, k) for k in range(1, SIDE)]
    held = (
        call(join_kernel, st((2, ROWS, WIDE), BF16), [VMEM] * 2, VMEM, 1000, *near[:2]),
        jnp.stack(near[2:]),
    )
    ll, lh, rl, rh, fl, fh = relay(*held, along_a)
    owners, slots, lens = page_owner[None], page_slot[None], cached_len[None]

    acc = call(
        project_first, st((ROWS, HD), F32), [SMEM] + [VMEM] * 3, VMEM, 70_000_000,
        info, *held, kv_weight,
    )
    acc = call(
        project_near, st((ROWS, HD), F32), [SMEM] + [VMEM] * 6, VMEM, 140_000_000,
        info, acc, ll, lh, rl, rh, kv_weight,
    )
    kv = call(
        project_far, st((ROWS, HD), BF16), [SMEM] + [VMEM] * 4, VMEM, 70_000_000,
        info, acc, fl, fh, kv_weight,
    )

    kv, queries = lax.optimization_barrier((kv, queries))
    other_queries = swap(queries)
    pair = routed(kv, both, lambda g, c, t: (g, c, t ^ 1))
    swapped = swap(kv)
    cross = routed(kv, both, lambda g, c, t: (1 - g, c, t ^ 1))
    cached = call(
        cache_rows, st((HALF // BLOCK, BLOCK, HD, 2 * HD), BF16), [SMEM, VMEM, HBM], VMEM, 1000,
        info, queries, cache, scratch=[dma((HALF // BLOCK,))], limit=49 << 20,
    )
    pair, cached = lax.optimization_barrier((pair, cached))
    span, new, part = call(
        pack_kernel, [st((2, ROWS, HD), BF16)] * 2 + [st((ROWS, HD), BF16)],
        [SMEM] + [VMEM] * 4, [VMEM] * 3, 1000, info, kv, pair, swapped, cross,
    )

    def along_z(block, k):
        return routed(
            block, both, lambda g, c, t: (g, (c + (k if g == 0 else NCTX - k)) % NCTX, t)
        )

    zs = [along_z(x, k) for k, x in ((1, span), (2, span), (3, span), (4, part))]
    tied, zs[3] = lax.optimization_barrier((queries, zs[3]))
    old = call(
        cache_kernel, st((2, 2, HALF, HD), F32), [SMEM] + [VMEM] * 6, VMEM, 1000,
        info, tied, other_queries, cached, lens, owners, slots,
        scratch=[pltpu.VMEM((HALF, 2 * HD), BF16), pltpu.VMEM((ROWS, HD), F32)],
    )
    other_old = swap(old)

    rs = [swap(z) for z in zs]
    small = st((2, ROWS, WIDE), BF16)
    att, s2l, s2h = call(
        finish_kernel, [st((ROWS, 2 * HD), BF16), small, small],
        [SMEM] + [VMEM] * 17, [VMEM] * 3, 300_000_000,
        info, queries, span, new, *zs, *rs, lens, owners, slots, old, other_old, out_weight,
    )
    s0, s1l, s1h, s3l, s3h = call(
        output_kernel, [st((SIDE, ROWS, WIDE), F32)] + [small] * 4,
        [SMEM, VMEM, VMEM], [VMEM] * 5, 400_000_000, info, att, out_weight,
    )
    to_right = shift(s2l, 1, 0)
    to_left = shift(s2h, -1, 0)
    lh = shift(s1h, 1, 0)
    rl = shift(s3l, -1, 0)
    add = lambda x, y: call(add_kernel, small, [VMEM] * 2, VMEM, 1000, x, y)
    ll = shift(add(s1l, to_right), 1, 0)
    rh = shift(add(s3h, to_left), -1, 0)
    line = call(fold_kernel, [small] * 2, [VMEM] * 5, [VMEM] * 2, 1000, s0, ll, lh, rl, rh)
    line = call(
        line_kernel, [small] * 2, [VMEM] * 8, [VMEM] * 2, 1000, *line, *relay(*line, along_b)
    )
    ll, lh, rl, rh, fl, fh = relay(*line, along_a)
    whole = st((ROWS, RANKS * WIDE), BF16)
    out = call(
        place_near, whole, [SMEM] + [VMEM] * 6, HBM, 1000, info, *line, ll, lh, rl, rh,
        scratch=[dma((3 * SIDE,))],
    )
    for kernel, far in ((place_low, fl), (place_high, fh)):
        out = call(
            kernel, whole, [SMEM, HBM, VMEM], HBM, 1000, info, out, far, scratch=[dma((2,))],
            aliases={1: 0},
        )
    return out[None]


def solution(mesh):
    return jax.shard_map(
        body,
        mesh=mesh,
        in_specs=(
            P("group", "ctx", "tp"),
            P("group", "ctx", "tp"),
            P(None, "tp"),
            P("tp", None),
            P("ctx", None, "tp"),
            P(),
            P(),
            P("ctx"),
        ),
        out_specs=P("group", "ctx", None),
        check_vma=False,
    )
```
